512 devices in a mesh: dp: 4 (over z_hi, core), ep: 32 (over z_lo, y), tp: 4 (over x).
Axes of the slice: x: 4, y: 4, z: 16 (z_hi: 2, z_lo: 8; z = z_hi * 8 + z_lo), core: 2. Of those that a mesh axis runs over, the one named last changes fastest.
Arguments:
- tokens: bfloat16 [2, 8192, 4096], P(None, ('dp', 'ep')), may hold values from -6 to 6
- expert_ids: int32 [2, 8192, 8], P(None, ('dp', 'ep')), may hold values from 0 to 31, as said below
- slot_index: int32 [2, 8192, 8], P(None, ('dp', 'ep')), may hold values from -1 to 17, as said below
- gate_weights: float32 [2, 8192, 8], P(None, ('dp', 'ep')), may hold values from 0.02 to 0.3
- up_gradient: bfloat16 [4, 2, 32, 576, 1536], P('dp', None, 'ep', None, 'tp'), may hold values from -6 to 6
- up_weight: bfloat16 [32, 4096, 1536], P('ep', 'tp', 'dp'), may hold values from -0.09375 to 0.09375
- attention_partial: bfloat16 [4, 2, 8192, 4096], P('tp', None, ('dp', 'ep')), may hold values from -6 to 6
- residual_gradient: bfloat16 [2, 8192, 4096], P(None, ('dp', 'ep'), 'tp'), may hold values from -6 to 6
Outputs:
- token_gradient: bfloat16 [2, 8192, 4096], P(None, ('dp', 'ep'), 'tp')
- weight_gradient: bfloat16 [32, 4096, 1536], P('ep', 'tp', 'dp')
The draws below stay inside these ranges and needn't reach their ends.
Inputs may be any that keep to these rules, and one draw needn't show every extreme that they name: `expert_ids`: each token names 8 different experts. `slot_index`: within the rows of one device and one micro-batch no two routes share an expert and a slot, and the kept routes of an expert take slots 0, 1, 2 and so on; -1 marks a dropped route. In every micro-batch some expert fills all 18 slots of every device.
All inputs are finite; a program needn't handle non-finite values.
Results may differ from the reference program's by a relative error of at most 0.013.
Values may be sent and summed in bfloat16 or wider, within the bound.
No kernel may reach another device: no remote copies, remote signals or barrier semaphores. Data moves between devices by JAX's collectives and lax.ppermute only.
A program may use at most 64 MiB of HBM per device.

```python
import math
import jax
import jax.numpy as jnp
from jax import lax

D = 4096
FF = 1536
TOK_DEV = 64
MB = 2
EXPERTS = 32
TOPK = 8
CAP = 18
ROWS = 576
TOKENS = 8192
REPLICAS = 4
SHARES = 4
N_DP = 4
N_EP = 32


def routing_pair(key):
    groups = TOKENS // TOK_DEV
    jitter_key, prefer_key, busy_key, order_key = jax.random.split(key, 4)
    jitter = jax.random.randint(jitter_key, (MB, groups, TOK_DEV, EXPERTS), 0, 1024)
    preference = jax.random.randint(prefer_key, (MB, groups, 1, EXPERTS), 0, 768)
    busy_expert = jax.random.randint(busy_key, (MB, 1, 1, 1), 0, EXPERTS)
    labels = jnp.arange(EXPERTS, dtype=jnp.int32)
    row_iota = jnp.arange(TOK_DEV, dtype=jnp.int32)
    order_score = jax.random.randint(order_key, (MB, groups, TOK_DEV), 0, 1 << 20) * TOK_DEV + row_iota
    order = jnp.argsort(order_score, axis=-1, stable=True)
    rank = jnp.argsort(order, axis=-1, stable=True).astype(jnp.int32)
    forced = ((labels == busy_expert) & (rank[..., None] < CAP)).astype(jnp.int32)
    scores = (jitter + preference + forced * 4096) * EXPERTS + labels
    picked = lax.top_k(scores, TOPK)[1].astype(jnp.int32)
    member = (picked[..., None] == labels).astype(jnp.int32).reshape(MB, groups, TOK_DEV * TOPK, EXPERTS)
    before = jnp.cumsum(member, axis=2) - member
    earlier = jnp.sum(before * member, axis=3).reshape(MB, groups, TOK_DEV, TOPK)
    slot_value = jnp.where(earlier < CAP, earlier, -1).astype(jnp.int32)
    return (picked.reshape(MB, TOKENS, TOPK), slot_value.reshape(MB, TOKENS, TOPK))


def draw_expert_ids(key, part):
    return routing_pair(key)[0]


def draw_slot_index(key, part):
    return routing_pair(key)[1]


def steps_of(key, shape, shards, smallest, top_value):
    def one(dim, shards_of):
        heights = jax.random.uniform(jax.random.fold_in(jax.random.fold_in(key, 6), dim), (shards_of,), jnp.float32, smallest / len(shards), top_value / len(shards))
        return jnp.repeat(jnp.exp(heights), shape[dim] // shards_of).reshape((-1,) + (1,) * (len(shape) - dim - 1))

    loudness = one(*shards[0])
    for cut in shards[1:]:
        loudness = loudness * one(*cut)
    return loudness


def scatter_about(own_key, shape, width, bound, cuts=(), kind=jnp.bfloat16):
    result = width * jax.random.normal(own_key, shape, jnp.float32)
    if cuts:
        result = result * steps_of(own_key, shape, cuts, -0.22, 0.18)
    return jnp.clip(result, -bound, bound).astype(kind)


def setup_inputs(seed: int = 0) -> dict:
    arg_keys = jax.random.split(jax.random.key(seed), 9)
    tokens = scatter_about(arg_keys[0], (MB, TOKENS, D), 1.0, 6.0, ((1, 128),))
    expert_ids = draw_expert_ids(jax.random.fold_in(arg_keys[8], 71), 0)
    slot_index = draw_slot_index(jax.random.fold_in(arg_keys[8], 71), 0)
    gate_weights = jnp.clip(jnp.exp(math.log(0.3) - 2.7080503 * jax.random.uniform(arg_keys[3], (MB, TOKENS, TOPK), jnp.float32) ** steps_of(arg_keys[3], (MB, TOKENS, TOPK), ((1, 128),), -0.2, 0.2)), 0.02, 0.3)
    up_gradient = scatter_about(arg_keys[4], (REPLICAS, MB, EXPERTS, ROWS, FF), 1.0, 6.0, ((0, 4), (2, 32), (4, 4)))
    up_weight = scatter_about(arg_keys[5], (EXPERTS, D, FF), D ** -0.5, 0.09375, ((0, 32), (1, 4), (2, 4)))
    attention_partial = scatter_about(arg_keys[6], (SHARES, MB, TOKENS, D), 0.5, 6.0, ((0, 4), (2, 128)))
    residual_gradient = scatter_about(arg_keys[7], (MB, TOKENS, D), 1.0, 6.0, ((1, 128), (2, 4)))
    return dict(tokens=tokens, expert_ids=expert_ids, slot_index=slot_index, gate_weights=gate_weights, up_gradient=up_gradient, up_weight=up_weight, attention_partial=attention_partial, residual_gradient=residual_gradient)


def reference(tokens, expert_ids, slot_index, gate_weights, up_gradient, up_weight, attention_partial, residual_gradient):
    blocks = tokens.reshape(MB, N_DP, N_EP, TOK_DEV, D)
    chosen = expert_ids.reshape(MB, N_DP, N_EP, TOK_DEV, TOPK)
    places = slot_index.reshape(MB, N_DP, N_EP, TOK_DEV, TOPK)
    weights = gate_weights.reshape(MB, N_DP, N_EP, TOK_DEV, TOPK)
    slot_iota = jnp.arange(CAP, dtype=jnp.int32)
    expert_iota = jnp.arange(EXPERTS, dtype=jnp.int32)
    grads_by_expert = jnp.moveaxis(up_gradient, 2, 0)

    def per_expert(carry, inputs):
        expert, up_rows, grads = inputs
        total = jnp.zeros((D, FF), jnp.float32)
        for replica in range(N_DP):
            partial_sum = jnp.zeros((D, FF), jnp.float32)
            for batch_index in range(MB):
                hits = (chosen[batch_index, replica] == expert) & (places[batch_index, replica] >= 0)
                picks = (places[batch_index, replica][..., None] == slot_iota) & hits[..., None]
                gate_table = jnp.sum(jnp.where(picks, weights[batch_index, replica][..., None], 0.0), axis=2)
                source = blocks[batch_index, replica].astype(jnp.float32)
                sent = jnp.einsum("btc,btd->bcd", gate_table, source, precision=lax.Precision.HIGHEST)
                sent = sent.astype(jnp.bfloat16).reshape(N_EP * CAP, D)
                back = jnp.dot(grads[replica, batch_index], up_rows.T, preferred_element_type=jnp.float32).astype(jnp.bfloat16)
                back_rows = back.reshape(N_EP, CAP, D).astype(jnp.float32)
                addition = jnp.einsum("btc,bcd->btd", gate_table, back_rows, precision=lax.Precision.HIGHEST)
                carry = carry.at[batch_index, replica].add(addition)
                partial_sum = partial_sum + jnp.dot(sent.T, grads[replica, batch_index], preferred_element_type=jnp.float32)
            rounded = lax.optimization_barrier(partial_sum.astype(jnp.bfloat16))
            total = total + rounded.astype(jnp.float32)
        weight_out = (total * (1.0 / N_DP)).astype(jnp.bfloat16)
        return carry, weight_out

    start = jnp.zeros((MB, N_DP, N_EP, TOK_DEV, D), jnp.float32)
    moe_sum, weight_gradient = lax.scan(per_expert, start, (expert_iota, up_weight, grads_by_expert))
    expert_part = moe_sum.reshape(MB, TOKENS, D)
    attention_total = jnp.sum(attention_partial.astype(jnp.float32), axis=0)
    token_gradient = (residual_gradient.astype(jnp.float32) + attention_total + expert_part).astype(jnp.bfloat16)
    return token_gradient, weight_gradient
```

```python
import jax
import jax.numpy as jnp
from jax import lax
from jax.sharding import Mesh, PartitionSpec as P

AXES = ("zh", "co", "zl", "y", "x")
SIZES = (2, 2, 8, 4, 4)
SWAP = [(0, 1), (1, 0)]


def slot_tables(expert_ids, slot_index, gate_weights, capacity, places):
    rows = expert_ids.shape[1]
    position = jnp.where(slot_index >= 0, expert_ids * capacity + slot_index, -1)
    matches = position[..., None] == jnp.arange(places, dtype=jnp.int32)
    token = jnp.arange(1, rows + 1, dtype=jnp.float32)[None, :, None, None]
    held = jnp.sum(jnp.where(matches, token, 0.0), axis=(1, 2)) - 1.0
    gate = jnp.sum(jnp.where(matches, gate_weights[..., None], 0.0), axis=(1, 2))
    return held, gate


def on_device(
    tokens,
    expert_ids,
    slot_index,
    gate_weights,
    up_gradient,
    up_weight,
    attention_partial,
    residual_gradient,
):
    nzl, ny, nx = (lax.axis_size(a) for a in ("zl", "y", "x"))
    zh, co, x = (lax.axis_index(a) for a in ("zh", "co", "x"))
    batches, held_tokens, width = tokens.shape
    quarter = width // nx
    buffer_rows, ff_part = up_gradient.shape[3:]
    capacity = buffer_rows // (nzl * ny)
    group = nzl * batches * capacity
    rows = ny * group
    bf16, f32 = jnp.bfloat16, jnp.float32

    own_part = lax.dynamic_slice_in_dim(tokens, x * quarter, quarter, 2)
    line = lax.all_gather(
        own_part.reshape(batches * held_tokens, quarter), "zl", axis=0, tiled=True
    )

    own = up_weight[0]
    across = lax.ppermute(own, "zh", SWAP)

    held, gate = slot_tables(
        expert_ids, slot_index, gate_weights, capacity, nzl * ny * capacity
    )
    table = jnp.stack([held, gate]).reshape(2, batches, nzl, ny * capacity)
    table = lax.all_to_all(
        table.transpose(2, 0, 1, 3), "zl", split_axis=0, concat_axis=0, tiled=True
    )
    table = table.reshape(nzl, 2, batches, ny, capacity).transpose(1, 3, 2, 0, 4)
    held = table[0].astype(jnp.int32)
    start = (
        jnp.arange(nzl, dtype=jnp.int32)[None, None, :, None] * (batches * held_tokens)
        + jnp.arange(batches, dtype=jnp.int32)[None, :, None, None] * held_tokens
    )
    column = jnp.where(held >= 0, held + start, -1).reshape(rows)
    slot_gate = table[1].reshape(rows)
    column_iota = jnp.arange(nzl * batches * held_tokens, dtype=jnp.int32)

    r = jnp.arange(rows, dtype=jnp.int32)
    r_slot = r % capacity
    r_zl = (r // capacity) % nzl
    r_batch = (r // (capacity * nzl)) % batches
    r_y = r // group
    source_row = ((r_batch * nzl + r_zl) * ny + r_y) * capacity + r_slot
    order = (source_row[:, None] == r[None, :]).astype(bf16)
    hidden = jnp.dot(
        order, up_gradient.reshape(rows, ff_part), preferred_element_type=f32
    ).astype(bf16)
    hidden = lax.all_to_all(
        jnp.broadcast_to(hidden, (nx, rows, ff_part)),
        "x",
        split_axis=0,
        concat_axis=0,
        tiled=True,
    )

    shares = attention_partial.reshape(batches * held_tokens, nx, quarter)
    shares = lax.all_to_all(
        shares.transpose(1, 0, 2), "x", split_axis=0, concat_axis=0, tiled=True
    )
    base = residual_gradient.reshape(batches * held_tokens, quarter).astype(f32) + jnp.sum(
        shares.astype(f32), axis=0
    )

    pick = (column[:, None] == column_iota[None, :]).astype(bf16)
    sent = jnp.dot(pick, line, preferred_element_type=f32) * slot_gate[:, None]
    inbound = lax.all_to_all(
        sent.astype(bf16).reshape(ny, group, quarter),
        "y",
        split_axis=0,
        concat_axis=0,
        tiled=True,
    ).reshape(rows, quarter)

    def part_of(a, b):
        return lax.dynamic_index_in_dim(hidden, 2 * a + b, 0, keepdims=False)

    beside = lax.ppermute(own, "co", SWAP)
    diagonal = lax.ppermute(across, "co", SWAP)
    back = jnp.zeros((rows, quarter), f32)
    for a, b, weight in (
        (zh, co, own),
        (zh, 1 - co, beside),
        (1 - zh, co, across),
        (1 - zh, 1 - co, diagonal),
    ):
        back = back + jnp.einsum("rf,df->rd", part_of(a, b), weight, preferred_element_type=f32)
    returned = lax.all_to_all(
        back.astype(bf16).reshape(ny, group, quarter),
        "y",
        split_axis=0,
        concat_axis=0,
        tiled=True,
    ).reshape(rows, quarter)

    def grad_of(a, b):
        return jnp.einsum("rd,rf->df", inbound, part_of(a, b), preferred_element_type=f32)

    other_far = lax.ppermute(grad_of(1 - zh, 1 - co).astype(bf16), "co", SWAP)
    other_near = lax.ppermute(grad_of(zh, 1 - co).astype(bf16), "co", SWAP)
    far = grad_of(1 - zh, co) + other_far.astype(f32)
    far = lax.ppermute(far.astype(bf16), "zh", SWAP)
    near = grad_of(zh, co) + other_near.astype(f32)
    weight_gradient = ((near + far.astype(f32)) * 0.25).astype(bf16)

    gate_high = lax.reduce_precision(slot_gate, 8, 7)
    gate_low = slot_gate - gate_high
    mine = column[None, :] == column_iota[:, None]
    spread = jnp.dot(
        jnp.where(mine, gate_high[None, :], 0.0).astype(bf16),
        returned,
        preferred_element_type=f32,
    ) + jnp.dot(
        jnp.where(mine, gate_low[None, :], 0.0).astype(bf16),
        returned,
        preferred_element_type=f32,
    )
    expert_part = lax.psum_scatter(spread.astype(bf16), "zl", scatter_dimension=0, tiled=True)
    token_gradient = (base + expert_part.astype(f32)).astype(bf16)
    return (
        token_gradient.reshape(batches, held_tokens, quarter),
        weight_gradient[None],
    )


def solution(mesh):
    split = Mesh(mesh.devices.reshape(SIZES), AXES)
    dp, ep, tp = ("zh", "co"), ("zl", "y"), "x"
    return jax.shard_map(
        on_device,
        mesh=split,
        in_specs=(
            P(None, dp + ep, None),
            P(None, dp + ep, None),
            P(None, dp + ep, None),
            P(None, dp + ep, None),
            P(dp, None, ep, None, tp),
            P(ep, tp, dp),
            P(tp, None, dp + ep, None),
            P(None, dp + ep, tp),
        ),
        out_specs=(P(None, dp + ep, tp), P(ep, tp, dp)),
        check_vma=False,
    )
```

```python
import jax
import jax.numpy as jnp
from jax import lax
from jax.experimental import pallas as pl
from jax.experimental.pallas import tpu as pltpu
from jax.sharding import Mesh, PartitionSpec as P

AXES = ("zh", "co", "zl", "y", "x")
SIZES = (2, 2, 8, 4, 4)
SWAP = [(0, 1), (1, 0)]
BF16, F32, I32 = jnp.bfloat16, jnp.float32, jnp.int32
VMEM = 48 * 1024 * 1024


def dot(a, b, over):
    return lax.dot_general(a, b, ((over[:1], over[1:]), ((), ())), preferred_element_type=F32)


def call(body, grid, in_specs, out_spec, out_shape, prefetch, flops, scratch=()):
    return pl.pallas_call(
        body,
        grid_spec=pltpu.PrefetchScalarGridSpec(
            num_scalar_prefetch=prefetch,
            grid=grid,
            in_specs=in_specs,
            out_specs=out_spec,
            scratch_shapes=scratch,
        ),
        out_shape=out_shape,
        compiler_params=pltpu.CompilerParams(vmem_limit_bytes=VMEM),
        cost_estimate=pl.CostEstimate(flops=flops, bytes_accessed=1 << 23, transcendentals=0),
    )


def pick_rows(half, line, table, far):
    batches, tok, width = line.shape[1:]
    width //= 2
    rows = table.shape[1]
    part = rows // SIZES[3]

    def body(zh_ref, line_ref, table_ref, out_ref):
        source = line_ref[...].reshape(8 * tok, width)
        seat = table_ref[0, :, 0:1].astype(I32)
        hit = seat == lax.broadcasted_iota(I32, (rows, 8 * tok), 1)
        taken = dot(jnp.where(hit, 1.0, 0.0).astype(BF16), source, (1, 0))
        taken = (taken * table_ref[0, :, 1:2]).astype(BF16)
        out_ref[...] = taken.reshape(out_ref.shape)

    return call(
        body,
        (2, batches),
        [
            pl.BlockSpec((8, 1, tok, width), lambda k, m, zh: (zh[0] ^ half, m, 0, k)),
            pl.BlockSpec((1, rows, 2), lambda k, m, zh: (half * 4 + k * 2 + m, 0, 0)),
        ],
        pl.BlockSpec((4, 1, 1, part, width), lambda k, m, zh: (0, k, m, 0, 0)),
        jax.ShapeDtypeStruct((4, 2, batches, part, width), BF16),
        1,
        8 * rows * 8 * tok * width,
    )(far, line, table)


def rows_back(near, other, weight):
    pairs, quarters, rows, ff = near.shape
    width = weight.shape[1]
    part = rows // 2

    def body(near_ref, other_ref, weight_ref, out_ref):
        for k, ref in enumerate((near_ref, other_ref)):
            total = dot(ref[0, 0], weight_ref[0], (1, 1)) + dot(ref[0, 1], weight_ref[1], (1, 1))
            total = total.astype(BF16)
            out_ref[0, k] = total[:part]
            out_ref[1, k] = total[part:]

    piece = pl.BlockSpec((1, quarters, rows, ff), lambda h: (h, 0, 0, 0))
    return call(
        body,
        (pairs,),
        [piece, piece, pl.BlockSpec(weight.shape, lambda h: (0, 0, 0))],
        pl.BlockSpec((2, 2, part, width), lambda h: (h, 0, 0, 0)),
        jax.ShapeDtypeStruct((4, 2, part, width), BF16),
        0,
        8 * pairs * rows * ff * width,
    )(near, other, weight)


def combine(near, far_rows, table, far, tok):
    _, _, batches, part, width = near.shape
    rows = 4 * part

    def body(zh_ref, near_ref, far_ref, table_ref, out_ref):
        seat = table_ref[0, 0:1, :].astype(I32)
        hit = seat == lax.broadcasted_iota(I32, (8 * tok, rows), 0)
        gate = jnp.where(hit, table_ref[0, 1:2, :], 0.0)
        high = gate.astype(BF16)
        low = (gate - high.astype(F32)).astype(BF16)

        def put(ref):
            source = ref[...].reshape(rows, width)
            total = dot(high, source, (1, 0)) + dot(low, source, (1, 0))
            out_ref[...] = total.astype(BF16).reshape(out_ref.shape)

        pl.when(pl.program_id(0) == 0)(lambda: put(near_ref))
        pl.when(pl.program_id(0) == 1)(lambda: put(far_ref))

    block = (4, 1, 1, part, width)
    return call(
        body,
        (2, 2, batches),
        [
            pl.BlockSpec(
                block,
                lambda j, k, m, zh: (0, jnp.where(j == 0, k, 1), jnp.where(j == 0, m, 1), 0, 0),
            ),
            pl.BlockSpec(
                block,
                lambda j, k, m, zh: (0, jnp.where(j == 0, 0, k), jnp.where(j == 0, 0, m), 0, 0),
            ),
            pl.BlockSpec((1, 2, rows), lambda j, k, m, zh: (j * 4 + k * 2 + m, 0, 0)),
        ],
        pl.BlockSpec((1, 8, 1, tok, width), lambda j, k, m, zh: (zh[0] ^ j, 0, m, 0, k)),
        jax.ShapeDtypeStruct((2, 8, batches, tok, 2 * width), BF16),
        1,
        32 * rows * 8 * tok * width,
    )(far, near, far_rows, table)


def weight_sum(inbound, near, other, so_far, scale, kind):
    count, _, part, width = inbound.shape
    quarters, ff = near.shape[1], near.shape[3]

    def body(in_ref, near_ref, other_ref, *refs):
        out_ref, total = refs[-2:]

        @pl.when(pl.program_id(0) == 0)
        def _():
            total[...] = jnp.zeros_like(total) if so_far is None else refs[0][...]

        for q in range(quarters):
            total[q] += dot(in_ref[0, 0], near_ref[0, q], (0, 0)) + dot(
                in_ref[0, 1], other_ref[0, q], (0, 0)
            )

        @pl.when(pl.program_id(0) == count - 1)
        def _():
            out_ref[...] = (total[...] * scale).astype(kind)

    piece = pl.BlockSpec((1, quarters, part, ff), lambda y: (y // 2, 0, y % 2, 0))
    whole = pl.BlockSpec((quarters, width, ff), lambda y: (0, 0, 0))
    extra = () if so_far is None else (so_far,)
    return call(
        body,
        (count,),
        [pl.BlockSpec((1, 2, part, width), lambda y: (y, 0, 0, 0)), piece, piece]
        + [whole] * len(extra),
        whole,
        jax.ShapeDtypeStruct((quarters, width, ff), kind),
        0,
        4 * count * part * width * quarters * ff,
        (pltpu.VMEM((quarters, width, ff), F32),),
    )(inbound, near, other, *extra)


def slot_tables(expert_ids, slot_index, gate_weights, capacity, places):
    rows = expert_ids.shape[1]
    position = jnp.where(slot_index >= 0, expert_ids * capacity + slot_index, -1)
    matches = position[..., None] == jnp.arange(places, dtype=I32)
    token = jnp.arange(1, rows + 1, dtype=F32)[None, :, None, None]
    held = jnp.sum(jnp.where(matches, token, 0.0), axis=(1, 2)) - 1.0
    gate = jnp.sum(jnp.where(matches, gate_weights[..., None], 0.0), axis=(1, 2))
    return held, gate


def by(flag, a, b):
    return jnp.where(flag == 0, a, b), jnp.where(flag == 0, b, a)


def on_device(
    tokens,
    expert_ids,
    slot_index,
    gate_weights,
    up_gradient,
    up_weight,
    attention_partial,
    residual_gradient,
):
    nzl, ny, nx = (lax.axis_size(a) for a in ("zl", "y", "x"))
    zh, co, x = (lax.axis_index(a) for a in ("zh", "co", "x"))
    batches, tok, width = tokens.shape
    quarter, eighth = width // nx, width // nx // 2
    buffer_rows, ff = up_gradient.shape[3:]
    capacity = buffer_rows // (nzl * ny)
    rows = batches * buffer_rows
    far = zh.astype(I32).reshape(1)

    def gather(v):
        return lax.all_to_all(
            jnp.broadcast_to(v, (nx,) + v.shape), "x", split_axis=0, concat_axis=0, tiled=True
        ).reshape((2, 2) + v.shape)

    def along_y(v):
        shape = v.shape
        v = v.reshape(ny, -1, shape[-1])
        return lax.all_to_all(v, "y", split_axis=0, concat_axis=0, tiled=True).reshape(shape)

    own_part = lax.dynamic_slice_in_dim(tokens, x * quarter, quarter, 2)
    own_part = own_part.reshape(batches * tok, 2, eighth)
    mine, theirs = by(co, own_part[:, 0], own_part[:, 1])
    line = jnp.concatenate([mine, lax.ppermute(theirs, "co", SWAP)], axis=1)
    line = lax.all_gather(line, ("zh", "zl"), axis=0, tiled=True)
    line = line.reshape(2 * nzl, batches, tok, quarter)

    r = jnp.arange(rows, dtype=I32)
    r_batch = (r // (capacity * nzl)) % batches
    source_row = (
        (r_batch * nzl + (r // capacity) % nzl) * ny + r // (capacity * nzl * batches)
    ) * capacity + r % capacity
    order = (source_row[:, None] == r[None, :]).astype(BF16)
    hidden = dot(order, up_gradient.reshape(rows, ff), (1, 0)).astype(BF16)
    halves = hidden.reshape(2, rows // 2, ff)
    xh = x // 2
    keep, send = by(xh, halves[0], halves[1])
    taken = lax.ppermute(send, "x", [(i, (i + 2) % nx) for i in range(nx)])
    stay, leave = by(xh ^ zh, keep, taken)
    crossed = lax.ppermute(leave, "zh", SWAP)

    held, gate = slot_tables(expert_ids, slot_index, gate_weights, capacity, nzl * ny * capacity)
    table = jnp.stack([held, gate]).reshape(2, batches, nzl, ny * capacity)
    table = table.transpose(2, 0, 1, 3)
    table = jnp.stack([table, lax.ppermute(table, "co", SWAP)], axis=1)
    table = lax.all_to_all(
        jnp.concatenate([table, table]), ("zh", "zl"), split_axis=0, concat_axis=0, tiled=True
    ).reshape(2, nzl, 2, 2, batches, ny, capacity)
    table = jnp.where(zh == 0, table, table[::-1])
    table = table.transpose(3, 0, 2, 4, 5, 1, 6)
    start = jnp.arange(nzl, dtype=F32)[:, None] * tok
    seats = jnp.where(table[0] >= 0, table[0] + start, -1.0)
    table = jnp.stack([seats, table[1]]).reshape(2, 4 * batches, buffer_rows)
    lying, standing = table.transpose(1, 0, 2), table.transpose(1, 2, 0)

    cut = up_weight.reshape(2, eighth, ff)
    mine, theirs = by(co, cut[0], cut[1])
    weight = jnp.stack(by(co, mine, lax.ppermute(theirs, "co", SWAP)))

    near = gather(stay)
    near_other = lax.ppermute(near, "co", SWAP)
    back_near = along_y(rows_back(near, near_other, weight))
    wide = gather(crossed)
    wide_other = lax.ppermute(wide, "co", SWAP)
    back_far = along_y(rows_back(wide, wide_other, weight))

    inbound = along_y(pick_rows(0, line, standing, far))
    inbound_far = along_y(pick_rows(1, line, standing, far))

    split = (4, 2, batches, nzl * capacity, eighth)
    spread = combine(back_near.reshape(split), back_far.reshape(split), lying, far, tok)
    expert_part = lax.psum_scatter(
        spread.reshape(2 * nzl * batches * tok, quarter),
        ("zh", "zl"),
        scatter_dimension=0,
        tiled=True,
    )

    split = (4, 2, batches * nzl * capacity, eighth)
    total = weight_sum(inbound.reshape(split), near, near_other, None, 1.0, F32)
    total = weight_sum(
        inbound_far.reshape(split), wide, wide_other, total, 1.0 / (2 * SIZES[1]), BF16
    )
    mine, theirs = by(co, total[0], total[1])
    weight_gradient = jnp.concatenate(by(co, mine, lax.ppermute(theirs, "co", SWAP)))

    shares = attention_partial.reshape(batches * tok, nx, quarter).transpose(1, 0, 2)
    shares = lax.all_to_all(shares, "x", split_axis=0, concat_axis=0, tiled=True)
    base = residual_gradient.reshape(batches * tok, quarter).astype(F32) + jnp.sum(
        shares.astype(F32), axis=0
    )
    other = lax.ppermute(expert_part[:, eighth:], "co", SWAP)
    expert_part = jnp.concatenate(by(co, expert_part[:, :eighth], other), axis=1)
    token_gradient = (base + expert_part.astype(F32)).astype(BF16)
    return (token_gradient.reshape(batches, tok, quarter), weight_gradient[None])


def solution(mesh):
    split = Mesh(mesh.devices.reshape(SIZES), AXES)
    dp, ep, tp = ("zh", "co"), ("zl", "y"), "x"
    return jax.shard_map(
        on_device,
        mesh=split,
        in_specs=(
            P(None, dp + ep, None),
            P(None, dp + ep, None),
            P(None, dp + ep, None),
            P(None, dp + ep, None),
            P(dp, None, ep, None, tp),
            P(ep, tp, dp),
            P(tp, None, dp + ep, None),
            P(None, dp + ep, tp),
        ),
        out_specs=(P(None, dp + ep, tp), P(ep, tp, dp)),
        check_vma=False,
    )
```

```python
import jax
import jax.numpy as jnp
from jax import lax
from jax.experimental import pallas as pl
from jax.experimental.pallas import tpu as pltpu
from jax.sharding import Mesh, PartitionSpec as P

AXES = ("zh", "co", "zl", "y", "x")
SIZES = (2, 2, 8, 4, 4)
SWAP = [(0, 1), (1, 0)]
BF16, F32, I32 = jnp.bfloat16, jnp.float32, jnp.int32
VMEM = 48 * 1024 * 1024


def dot(a, b, over):
    return lax.dot_general(a, b, ((over[:1], over[1:]), ((), ())), preferred_element_type=F32)


def call(body, grid, in_specs, out_spec, out_shape, prefetch, flops, scratch=(), aliases={}):
    return pl.pallas_call(
        body,
        grid_spec=pltpu.PrefetchScalarGridSpec(
            num_scalar_prefetch=prefetch,
            grid=grid,
            in_specs=in_specs,
            out_specs=out_spec,
            scratch_shapes=scratch,
        ),
        out_shape=out_shape,
        input_output_aliases=aliases,
        compiler_params=pltpu.CompilerParams(vmem_limit_bytes=VMEM),
        cost_estimate=pl.CostEstimate(flops=flops, bytes_accessed=1 << 23, transcendentals=0),
    )


def pick_rows(half, line, table, far):
    batches, tok, width = line.shape[1:]
    width //= 2
    rows = table.shape[1]
    part = rows // 4

    def body(zh_ref, line_ref, table_ref, *out_refs):
        source = line_ref[...].reshape(8 * tok, width)
        seat = table_ref[0, :, 0:1].astype(I32)
        hit = seat == lax.broadcasted_iota(I32, (rows, 8 * tok), 1)
        taken = dot(jnp.where(hit, 1.0, 0.0).astype(BF16), source, (1, 0))
        taken = (taken * table_ref[0, :, 1:2]).astype(BF16)
        for d, ref in enumerate(out_refs):
            ref[0, 0] = taken[d * part : (d + 1) * part]

    return call(
        body,
        (2, batches),
        [
            pl.BlockSpec((8, 1, tok, width), lambda k, m, zh: (zh[0] ^ half, m, 0, k)),
            pl.BlockSpec((1, rows, 2), lambda k, m, zh: (half * 4 + k * 2 + m, 0, 0)),
        ],
        [pl.BlockSpec((1, 1, part, width), lambda k, m, zh: (k, m, 0, 0))] * 4,
        [jax.ShapeDtypeStruct((2, batches, part, width), BF16)] * 4,
        1,
        8 * rows * 8 * tok * width,
    )(far, line, table)


def rows_back(near, other, weight, here):
    _, quarters, rows, ff = near.shape
    width = weight.shape[1]
    part = rows // 2

    def body(y_ref, near_ref, other_ref, weight_ref, *out_refs):
        for d, out_ref in enumerate(out_refs):

            @pl.when(pl.program_id(0) == d)
            def _():
                for k, ref in enumerate((near_ref, other_ref)):
                    total = dot(ref[0, 0], weight_ref[0], (1, 1))
                    total += dot(ref[0, 1], weight_ref[1], (1, 1))
                    out_ref[k] = total.astype(BF16)

    def place(d, y):
        source = (y[0] + d) & 3
        return (source >> 1, 0, source & 1, 0)

    piece = pl.BlockSpec((1, quarters, part, ff), place)
    return call(
        body,
        (4,),
        [piece, piece, pl.BlockSpec(weight.shape, lambda d, y: (0, 0, 0))],
        [pl.BlockSpec((2, part, width), lambda d, y: (0, 0, 0))] * 4,
        [jax.ShapeDtypeStruct((2, part, width), BF16)] * 4,
        1,
        16 * part * quarters * ff * width,
    )(here, near, other, weight)


def combine(half, returned, table, far, tok, so_far):
    returned = [returned[d] for d in (0, 3, 2, 1)]
    _, batches, part, width = returned[0].shape
    rows = 4 * part

    def body(zh_ref, *refs):
        out_ref, table_ref = refs[-1], refs[4]
        seat = table_ref[0, 0:1, :].astype(I32)
        hit = seat == lax.broadcasted_iota(I32, (8 * tok, rows), 0)
        gate = jnp.where(hit, table_ref[0, 1:2, :], 0.0)
        high = gate.astype(BF16)
        low = (gate - high.astype(F32)).astype(BF16)
        source = jnp.concatenate([ref[0, 0] for ref in refs[:4]], axis=0)
        total = dot(high, source, (1, 0)) + dot(low, source, (1, 0))
        out_ref[...] = total.astype(BF16).reshape(out_ref.shape)

    extra = () if so_far is None else (so_far,)
    return call(
        body,
        (2, batches),
        [pl.BlockSpec((1, 1, part, width), lambda k, m, zh: (k, m, 0, 0))] * 4
        + [pl.BlockSpec((1, 2, rows), lambda k, m, zh: (half * 4 + k * 2 + m, 0, 0))]
        + [pl.BlockSpec(memory_space=pl.ANY)] * len(extra),
        pl.BlockSpec((1, 8, 1, tok, width), lambda k, m, zh: (zh[0] ^ half, 0, m, 0, k)),
        jax.ShapeDtypeStruct((2, 8, batches, tok, 2 * width), BF16),
        1,
        16 * rows * 8 * tok * width,
        aliases={6: 0} if extra else {},
    )(far, *returned, table, *extra)


def weight_sum(inbound, near, other, here, so_far, scale, kind):
    _, part, width = inbound[0].shape
    quarters, ff = near.shape[1], near.shape[3]

    def body(y_ref, *refs):
        near_ref, other_ref = refs[4:6]
        out_ref, total = refs[-2:]

        @pl.when(pl.program_id(0) == 0)
        def _():
            total[...] = jnp.zeros_like(total) if so_far is None else refs[6][...]

        for d in range(4):

            @pl.when(pl.program_id(0) == d)
            def _():
                for q in range(quarters):
                    total[q] += dot(refs[d][0], near_ref[0, q], (0, 0)) + dot(
                        refs[d][1], other_ref[0, q], (0, 0)
                    )

        @pl.when(pl.program_id(0) == 3)
        def _():
            out_ref[...] = (total[...] * scale).astype(kind)

    def place(d, y):
        source = (y[0] - d) & 3
        return (source >> 1, 0, source & 1, 0)

    piece = pl.BlockSpec((1, quarters, part, ff), place)
    whole = pl.BlockSpec((quarters, width, ff), lambda d, y: (0, 0, 0))
    extra = () if so_far is None else (so_far,)
    return call(
        body,
        (4,),
        [pl.BlockSpec((2, part, width), lambda d, y: (0, 0, 0))] * 4
        + [piece, piece]
        + [whole] * len(extra),
        whole,
        jax.ShapeDtypeStruct((quarters, width, ff), kind),
        1,
        16 * part * width * quarters * ff,
        scratch=(pltpu.VMEM((quarters, width, ff), F32),),
    )(here, *inbound, near, other, *extra)


def slot_tables(expert_ids, slot_index, gate_weights, capacity, places):
    rows = expert_ids.shape[1]
    position = jnp.where(slot_index >= 0, expert_ids * capacity + slot_index, -1)
    matches = position[..., None] == jnp.arange(places, dtype=I32)
    token = jnp.arange(1, rows + 1, dtype=F32)[None, :, None, None]
    held = jnp.sum(jnp.where(matches, token, 0.0), axis=(1, 2)) - 1.0
    gate = jnp.sum(jnp.where(matches, gate_weights[..., None], 0.0), axis=(1, 2))
    return held, gate


def by(flag, a, b):
    return jnp.where(flag == 0, a, b), jnp.where(flag == 0, b, a)


def on_device(
    tokens,
    expert_ids,
    slot_index,
    gate_weights,
    up_gradient,
    up_weight,
    attention_partial,
    residual_gradient,
):
    nzl, ny, nx = (lax.axis_size(a) for a in ("zl", "y", "x"))
    zh, co, x = (lax.axis_index(a) for a in ("zh", "co", "x"))
    batches, tok, width = tokens.shape
    quarter, eighth = width // nx, width // nx // 2
    buffer_rows, ff = up_gradient.shape[3:]
    capacity = buffer_rows // (nzl * ny)
    rows = batches * buffer_rows
    far = zh.astype(I32).reshape(1)
    y = lax.axis_index("y")
    here = y.astype(I32).reshape(1)

    def gather(v):
        return lax.all_to_all(
            jnp.broadcast_to(v, (nx,) + v.shape), "x", split_axis=0, concat_axis=0, tiled=True
        ).reshape((2, 2) + v.shape)

    def along_y(parts, shape):
        moved = [
            v if d == 0 else lax.ppermute(v, "y", [(i, (i + d) % ny) for i in range(ny)])
            for d, v in enumerate(parts)
        ]
        return [v.reshape(shape) for v in moved]

    own_part = lax.dynamic_slice_in_dim(tokens, x * quarter, quarter, 2)
    own_part = own_part.reshape(batches * tok, 2, eighth)
    mine, theirs = by(co, own_part[:, 0], own_part[:, 1])
    line = jnp.concatenate([mine, lax.ppermute(theirs, "co", SWAP)], axis=1)
    line = lax.all_gather(line, ("zh", "zl"), axis=0, tiled=True)
    line = line.reshape(2 * nzl, batches, tok, quarter)

    r = jnp.arange(rows, dtype=I32)
    r_batch = (r // (capacity * nzl)) % batches
    source_row = (
        (r_batch * nzl + (r // capacity) % nzl) * ny + r // (capacity * nzl * batches)
    ) * capacity + r % capacity
    order = (source_row[:, None] == r[None, :]).astype(BF16)
    hidden = dot(order, up_gradient.reshape(rows, ff), (1, 0)).astype(BF16)
    halves = hidden.reshape(2, rows // 2, ff)
    xh = x // 2
    keep, send = by(xh, halves[0], halves[1])
    taken = lax.ppermute(send, "x", [(i, (i + 2) % nx) for i in range(nx)])
    stay, leave = by(xh ^ zh, keep, taken)
    crossed = lax.ppermute(leave, "zh", SWAP)
    near = gather(stay)

    expert_ids, slot_index, gate_weights, leave = lax.optimization_barrier(
        (expert_ids, slot_index, gate_weights, leave)
    )
    held, gate = slot_tables(expert_ids, slot_index, gate_weights, capacity, nzl * ny * capacity)
    table = jnp.stack([held, gate]).reshape(2, batches, nzl, ny * capacity)
    table = table.transpose(2, 0, 1, 3)
    table = jnp.stack([table, lax.ppermute(table, "co", SWAP)], axis=1)
    table = lax.all_to_all(
        jnp.concatenate([table, table]), ("zh", "zl"), split_axis=0, concat_axis=0, tiled=True
    ).reshape(2, nzl, 2, 2, batches, ny, capacity)
    table = jnp.where(zh == 0, table, table[::-1])
    table = lax.dynamic_slice_in_dim(jnp.concatenate([table, table], axis=5), y, ny, 5)
    table = table.transpose(3, 0, 2, 4, 5, 1, 6)
    start = jnp.arange(nzl, dtype=F32)[:, None] * tok
    seats = jnp.where(table[0] >= 0, table[0] + start, -1.0)
    table = jnp.stack([seats, table[1]]).reshape(2, 4 * batches, buffer_rows)
    lying, standing = table.transpose(1, 0, 2), table.transpose(1, 2, 0)

    cut = up_weight.reshape(2, eighth, ff)
    mine, theirs = by(co, cut[0], cut[1])
    weight = jnp.stack(by(co, mine, lax.ppermute(theirs, "co", SWAP)))

    near_other = lax.ppermute(near, "co", SWAP)
    back = rows_back(near, near_other, weight, here)
    crossed, back, lying, standing = lax.optimization_barrier((crossed, back, lying, standing))
    wide = gather(crossed)
    split = (2, batches, nzl * capacity, eighth)
    spread = combine(0, along_y(back, split), lying, far, tok, None)
    wide_other = lax.ppermute(wide, "co", SWAP)
    back = rows_back(wide, wide_other, weight, here)
    attention_partial, back = lax.optimization_barrier((attention_partial, back))
    spread = combine(1, along_y(back, split), lying, far, tok, spread)
    line, _ = lax.optimization_barrier((line, spread))
    expert_part = lax.psum_scatter(
        spread.reshape(2 * nzl * batches * tok, quarter),
        ("zh", "zl"),
        scatter_dimension=0,
        tiled=True,
    )

    split = (2, batches * nzl * capacity, eighth)
    inbound = along_y(pick_rows(0, line, standing, far), split)
    inbound_far = along_y(pick_rows(1, line, standing, far), split)
    total = weight_sum(inbound, near, near_other, here, None, 1.0, F32)
    total = weight_sum(inbound_far, wide, wide_other, here, total, 1.0 / (2 * SIZES[1]), BF16)
    mine, theirs = by(co, total[0], total[1])
    weight_gradient = jnp.concatenate(by(co, mine, lax.ppermute(theirs, "co", SWAP)))

    shares = attention_partial.reshape(batches * tok, nx, quarter).transpose(1, 0, 2)
    shares = lax.all_to_all(shares, "x", split_axis=0, concat_axis=0, tiled=True)
    base = residual_gradient.reshape(batches * tok, quarter).astype(F32) + jnp.sum(
        shares.astype(F32), axis=0
    )
    other = lax.ppermute(expert_part[:, eighth:], "co", SWAP)
    expert_part = jnp.concatenate(by(co, expert_part[:, :eighth], other), axis=1)
    token_gradient = (base + expert_part.astype(F32)).astype(BF16)
    return (token_gradient.reshape(batches, tok, quarter), weight_gradient[None])


def solution(mesh):
    split = Mesh(mesh.devices.reshape(SIZES), AXES)
    dp, ep, tp = ("zh", "co"), ("zl", "y"), "x"
    return jax.shard_map(
        on_device,
        mesh=split,
        in_specs=(
            P(None, dp + ep, None),
            P(None, dp + ep, None),
            P(None, dp + ep, None),
            P(None, dp + ep, None),
            P(dp, None, ep, None, tp),
            P(ep, tp, dp),
            P(tp, None, dp + ep, None),
            P(None, dp + ep, tp),
        ),
        out_specs=(P(None, dp + ep, tp), P(ep, tp, dp)),
        check_vma=False,
    )
```

```python
import jax
import jax.numpy as jnp
from jax import lax
from jax.experimental import pallas as pl
from jax.experimental.pallas import tpu as pltpu
from jax.sharding import Mesh, PartitionSpec as P

AXES = ("zh", "co", "zl", "y", "x")
SIZES = (2, 2, 8, 4, 4)
SWAP = [(0, 1), (1, 0)]
BF16, F32, I32 = jnp.bfloat16, jnp.float32, jnp.int32
VMEM = 48 * 1024 * 1024


def dot(a, b, over):
    return lax.dot_general(a, b, ((over[:1], over[1:]), ((), ())), preferred_element_type=F32)


def call(body, grid, in_specs, out_spec, out_shape, prefetch, flops, scratch=(), aliases={}):
    return pl.pallas_call(
        body,
        grid_spec=pltpu.PrefetchScalarGridSpec(
            num_scalar_prefetch=prefetch,
            grid=grid,
            in_specs=in_specs,
            out_specs=out_spec,
            scratch_shapes=scratch,
        ),
        out_shape=out_shape,
        input_output_aliases=aliases,
        compiler_params=pltpu.CompilerParams(vmem_limit_bytes=VMEM),
        cost_estimate=pl.CostEstimate(flops=flops, bytes_accessed=1 << 23, transcendentals=0),
    )


def pick_rows(half, line, table, far):
    batches, tok, width = line.shape[1:]
    width //= 2
    rows = table.shape[1]
    part = rows // 4

    def body(zh_ref, line_ref, table_ref, *out_refs):
        source = line_ref[...].reshape(8 * tok, width)
        seat = table_ref[0, :, 0:1].astype(I32)
        hit = seat == lax.broadcasted_iota(I32, (rows, 8 * tok), 1)
        taken = dot(jnp.where(hit, 1.0, 0.0).astype(BF16), source, (1, 0))
        taken = (taken * table_ref[0, :, 1:2]).astype(BF16)
        for d, ref in enumerate(out_refs):
            ref[0, 0] = taken[d * part : (d + 1) * part]

    return call(
        body,
        (2, batches),
        [
            pl.BlockSpec((8, 1, tok, width), lambda k, m, zh: (zh[0] ^ half, m, 0, k)),
            pl.BlockSpec((1, rows, 2), lambda k, m, zh: (half * 4 + k * 2 + m, 0, 0)),
        ],
        [pl.BlockSpec((1, 1, part, width), lambda k, m, zh: (k, m, 0, 0))] * 4,
        [jax.ShapeDtypeStruct((2, batches, part, width), BF16)] * 4,
        1,
        8 * rows * 8 * tok * width,
    )(far, line, table)


def rows_back(near, other, weight, here):
    _, quarters, rows, ff = near.shape
    width = weight.shape[1]
    part = rows // 2

    def body(y_ref, near_ref, other_ref, weight_ref, *out_refs):
        for d, out_ref in enumerate(out_refs):

            @pl.when(pl.program_id(0) == d)
            def _():
                for k, ref in enumerate((near_ref, other_ref)):
                    total = dot(ref[0, 0], weight_ref[0], (1, 1))
                    total += dot(ref[0, 1], weight_ref[1], (1, 1))
                    out_ref[k] = total.astype(BF16)

    def place(d, y):
        source = (y[0] + d) & 3
        return (source >> 1, 0, source & 1, 0)

    piece = pl.BlockSpec((1, quarters, part, ff), place)
    return call(
        body,
        (4,),
        [piece, piece, pl.BlockSpec(weight.shape, lambda d, y: (0, 0, 0))],
        [pl.BlockSpec((2, part, width), lambda d, y: (0, 0, 0))] * 4,
        [jax.ShapeDtypeStruct((2, part, width), BF16)] * 4,
        1,
        16 * part * quarters * ff * width,
    )(here, near, other, weight)


def combine(half, returned, table, far, tok, so_far):
    returned = [returned[d] for d in (0, 3, 2, 1)]
    _, batches, part, width = returned[0].shape
    rows = 4 * part

    def body(zh_ref, *refs):
        out_ref, table_ref = refs[-1], refs[4]
        seat = table_ref[0, 0:1, :].astype(I32)
        hit = seat == lax.broadcasted_iota(I32, (8 * tok, rows), 0)
        gate = jnp.where(hit, table_ref[0, 1:2, :], 0.0)
        high = gate.astype(BF16)
        low = (gate - high.astype(F32)).astype(BF16)
        source = jnp.concatenate([ref[0, 0] for ref in refs[:4]], axis=0)
        total = dot(high, source, (1, 0)) + dot(low, source, (1, 0))
        out_ref[...] = total.astype(BF16).reshape(out_ref.shape)

    extra = () if so_far is None else (so_far,)
    return call(
        body,
        (2, batches),
        [pl.BlockSpec((1, 1, part, width), lambda k, m, zh: (k, m, 0, 0))] * 4
        + [pl.BlockSpec((1, 2, rows), lambda k, m, zh: (half * 4 + k * 2 + m, 0, 0))]
        + [pl.BlockSpec(memory_space=pl.ANY)] * len(extra),
        pl.BlockSpec((1, 8, 1, tok, width), lambda k, m, zh: (zh[0] ^ half, 0, m, 0, k)),
        jax.ShapeDtypeStruct((2, 8, batches, tok, 2 * width), BF16),
        1,
        16 * rows * 8 * tok * width,
        aliases={6: 0} if extra else {},
    )(far, *returned, table, *extra)


def weight_sum(inbound, near, other, here, so_far, scale, kind):
    _, part, width = inbound[0].shape
    quarters, ff = near.shape[1], near.shape[3]

    def body(y_ref, *refs):
        near_ref, other_ref = refs[4:6]
        out_ref, total = refs[-2:]

        @pl.when(pl.program_id(0) == 0)
        def _():
            total[...] = jnp.zeros_like(total) if so_far is None else refs[6][...]

        for d in range(4):

            @pl.when(pl.program_id(0) == d)
            def _():
                for q in range(quarters):
                    total[q] += dot(refs[d][0], near_ref[0, q], (0, 0)) + dot(
                        refs[d][1], other_ref[0, q], (0, 0)
                    )

        @pl.when(pl.program_id(0) == 3)
        def _():
            out_ref[...] = (total[...] * scale).astype(kind)

    def place(d, y):
        source = (y[0] - d) & 3
        return (source >> 1, 0, source & 1, 0)

    piece = pl.BlockSpec((1, quarters, part, ff), place)
    whole = pl.BlockSpec((quarters, width, ff), lambda d, y: (0, 0, 0))
    extra = () if so_far is None else (so_far,)
    return call(
        body,
        (4,),
        [pl.BlockSpec((2, part, width), lambda d, y: (0, 0, 0))] * 4
        + [piece, piece]
        + [whole] * len(extra),
        whole,
        jax.ShapeDtypeStruct((quarters, width, ff), kind),
        1,
        16 * part * width * quarters * ff,
        scratch=(pltpu.VMEM((quarters, width, ff), F32),),
    )(here, *inbound, near, other, *extra)


def slot_tables(expert_ids, slot_index, gate_weights, capacity, places):
    rows = expert_ids.shape[1]
    position = jnp.where(slot_index >= 0, expert_ids * capacity + slot_index, -1)
    matches = position[..., None] == jnp.arange(places, dtype=I32)
    token = jnp.arange(1, rows + 1, dtype=F32)[None, :, None, None]
    held = jnp.sum(jnp.where(matches, token, 0.0), axis=(1, 2)) - 1.0
    gate = jnp.sum(jnp.where(matches, gate_weights[..., None], 0.0), axis=(1, 2))
    return held, gate


def by(flag, a, b):
    return jnp.where(flag == 0, a, b), jnp.where(flag == 0, b, a)


def on_device(
    tokens,
    expert_ids,
    slot_index,
    gate_weights,
    up_gradient,
    up_weight,
    attention_partial,
    residual_gradient,
):
    nzl, ny, nx = (lax.axis_size(a) for a in ("zl", "y", "x"))
    zh, co, x = (lax.axis_index(a) for a in ("zh", "co", "x"))
    batches, tok, width = tokens.shape
    quarter, eighth = width // nx, width // nx // 2
    buffer_rows, ff = up_gradient.shape[3:]
    capacity = buffer_rows // (nzl * ny)
    rows = batches * buffer_rows
    far = zh.astype(I32).reshape(1)
    y = lax.axis_index("y")
    here = y.astype(I32).reshape(1)

    def gather(v):
        return lax.all_to_all(
            jnp.broadcast_to(v, (nx,) + v.shape), "x", split_axis=0, concat_axis=0, tiled=True
        ).reshape((2, 2) + v.shape)

    def along_y(parts, shape):
        moved = [
            v if d == 0 else lax.ppermute(v, "y", [(i, (i + d) % ny) for i in range(ny)])
            for d, v in enumerate(parts)
        ]
        return [v.reshape(shape) for v in moved]

    own_part = lax.dynamic_slice_in_dim(tokens, x * quarter, quarter, 2)
    own_part = own_part.reshape(batches * tok, 2, eighth)
    mine, theirs = by(co, own_part[:, 0], own_part[:, 1])
    line = jnp.concatenate([mine, lax.ppermute(theirs, "co", SWAP)], axis=1)
    line = lax.all_gather(line, ("zh", "zl"), axis=0, tiled=True)
    line = line.reshape(2 * nzl, batches, tok, quarter)

    r = jnp.arange(rows, dtype=I32)
    r_batch = (r // (capacity * nzl)) % batches
    source_row = (
        (r_batch * nzl + (r // capacity) % nzl) * ny + r // (capacity * nzl * batches)
    ) * capacity + r % capacity
    order = (source_row[:, None] == r[None, :]).astype(BF16)
    hidden = dot(order, up_gradient.reshape(rows, ff), (1, 0)).astype(BF16)
    halves = hidden.reshape(2, rows // 2, ff)
    xh = x // 2
    keep, send = by(xh, halves[0], halves[1])
    taken = lax.ppermute(send, "x", [(i, (i + 2) % nx) for i in range(nx)])
    stay, leave = by(xh ^ zh, keep, taken)
    crossed = lax.ppermute(leave, "zh", SWAP)
    near = gather(stay)

    cut = up_weight.reshape(2, eighth, ff)
    mine, theirs = by(co, cut[0], cut[1])
    weight = jnp.stack(by(co, mine, lax.ppermute(theirs, "co", SWAP)))

    near_other = lax.ppermute(near, "co", SWAP)
    back = rows_back(near, near_other, weight, here)
    crossed, expert_ids, slot_index, gate_weights = lax.optimization_barrier(
        (crossed, expert_ids, slot_index, gate_weights)
    )
    wide = gather(crossed)
    wide, back = lax.optimization_barrier((wide, back))

    held, gate = slot_tables(expert_ids, slot_index, gate_weights, capacity, nzl * ny * capacity)
    table = jnp.stack([held, gate]).reshape(2, batches, nzl, ny * capacity)
    table = table.transpose(2, 0, 1, 3)
    table = jnp.stack([table, lax.ppermute(table, "co", SWAP)], axis=1)
    table, wide = lax.optimization_barrier((table, wide))
    table = lax.all_to_all(
        jnp.concatenate([table, table]), ("zh", "zl"), split_axis=0, concat_axis=0, tiled=True
    ).reshape(2, nzl, 2, 2, batches, ny, capacity)
    table = jnp.where(zh == 0, table, table[::-1])
    table = lax.dynamic_slice_in_dim(jnp.concatenate([table, table], axis=5), y, ny, 5)
    table = table.transpose(3, 0, 2, 4, 5, 1, 6)
    start = jnp.arange(nzl, dtype=F32)[:, None] * tok
    seats = jnp.where(table[0] >= 0, table[0] + start, -1.0)
    table = jnp.stack([seats, table[1]]).reshape(2, 4 * batches, buffer_rows)
    lying, standing = table.transpose(1, 0, 2), table.transpose(1, 2, 0)

    split = (2, batches, nzl * capacity, eighth)
    spread = combine(0, along_y(back, split), lying, far, tok, None)
    wide_other = lax.ppermute(wide, "co", SWAP)
    back = rows_back(wide, wide_other, weight, here)
    attention_partial, back = lax.optimization_barrier((attention_partial, back))
    spread = combine(1, along_y(back, split), lying, far, tok, spread)
    line, _ = lax.optimization_barrier((line, spread))
    expert_part = lax.psum_scatter(
        spread.reshape(2 * nzl * batches * tok, quarter),
        ("zh", "zl"),
        scatter_dimension=0,
        tiled=True,
    )

    split = (2, batches * nzl * capacity, eighth)
    inbound = along_y(pick_rows(0, line, standing, far), split)
    inbound_far = along_y(pick_rows(1, line, standing, far), split)
    total = weight_sum(inbound, near, near_other, here, None, 1.0, F32)
    total = weight_sum(inbound_far, wide, wide_other, here, total, 1.0 / (2 * SIZES[1]), BF16)
    mine, theirs = by(co, total[0], total[1])
    weight_gradient = jnp.concatenate(by(co, mine, lax.ppermute(theirs, "co", SWAP)))

    shares = attention_partial.reshape(batches * tok, nx, quarter).transpose(1, 0, 2)
    shares = lax.all_to_all(shares, "x", split_axis=0, concat_axis=0, tiled=True)
    base = residual_gradient.reshape(batches * tok, quarter).astype(F32) + jnp.sum(
        shares.astype(F32), axis=0
    )
    other = lax.ppermute(expert_part[:, eighth:], "co", SWAP)
    expert_part = jnp.concatenate(by(co, expert_part[:, :eighth], other), axis=1)
    token_gradient = (base + expert_part.astype(F32)).astype(BF16)
    return (token_gradient.reshape(batches, tok, quarter), weight_gradient[None])


def solution(mesh):
    split = Mesh(mesh.devices.reshape(SIZES), AXES)
    dp, ep, tp = ("zh", "co"), ("zl", "y"), "x"
    return jax.shard_map(
        on_device,
        mesh=split,
        in_specs=(
            P(None, dp + ep, None),
            P(None, dp + ep, None),
            P(None, dp + ep, None),
            P(None, dp + ep, None),
            P(dp, None, ep, None, tp),
            P(ep, tp, dp),
            P(tp, None, dp + ep, None),
            P(None, dp + ep, tp),
        ),
        out_specs=(P(None, dp + ep, tp), P(ep, tp, dp)),
        check_vma=False,
    )
```

```python
import jax
import jax.numpy as jnp
from jax import lax
from jax.experimental import pallas as pl
from jax.experimental.pallas import tpu as pltpu
from jax.sharding import Mesh, PartitionSpec as P

AXES = ("zh", "co", "zl", "y", "x")
SIZES = (2, 2, 8, 4, 4)
SWAP = [(0, 1), (1, 0)]
BF16, F32, I32 = jnp.bfloat16, jnp.float32, jnp.int32
VMEM = 48 * 1024 * 1024


def dot(a, b, over):
    return lax.dot_general(a, b, ((over[:1], over[1:]), ((), ())), preferred_element_type=F32)


def call(body, grid, in_specs, out_spec, out_shape, prefetch, flops, scratch=(), aliases={}):
    return pl.pallas_call(
        body,
        grid_spec=pltpu.PrefetchScalarGridSpec(
            num_scalar_prefetch=prefetch,
            grid=grid,
            in_specs=in_specs,
            out_specs=out_spec,
            scratch_shapes=scratch,
        ),
        out_shape=out_shape,
        input_output_aliases=aliases,
        compiler_params=pltpu.CompilerParams(vmem_limit_bytes=VMEM),
        cost_estimate=pl.CostEstimate(flops=flops, bytes_accessed=1 << 23, transcendentals=0),
    )


def pick_rows(half, line, table, far, width):
    batches, tok = line.shape[1:3]
    rows = table.shape[1]
    part = rows // 4

    def body(zh_ref, line_ref, table_ref, *out_refs):
        source = line_ref[...].reshape(8 * tok, width)
        seat = table_ref[0, :, 0:1].astype(I32)
        hit = seat == lax.broadcasted_iota(I32, (rows, 8 * tok), 1)
        taken = dot(jnp.where(hit, 1.0, 0.0).astype(BF16), source, (1, 0))
        taken = (taken * table_ref[0, :, 1:2]).astype(BF16)
        for d, ref in enumerate(out_refs):
            ref[0, 0] = taken[d * part : (d + 1) * part]

    return call(
        body,
        (2, batches),
        [
            pl.BlockSpec((8, 1, tok, width), lambda k, m, zh: (zh[0] ^ half, m, 0, k)),
            pl.BlockSpec((1, rows, 2), lambda k, m, zh: (half * 4 + k * 2 + m, 0, 0)),
        ],
        [pl.BlockSpec((1, 1, part, width), lambda k, m, zh: (k, m, 0, 0))] * 4,
        [jax.ShapeDtypeStruct((2, batches, part, width), BF16)] * 4,
        1,
        8 * rows * 8 * tok * width,
    )(far, line, table)


def rows_back(near, other, weight, here):
    _, quarters, batches, _, part, ff = near.shape
    width = weight.shape[1]
    shape = (2, batches, part, width)

    def body(y_ref, near_ref, other_ref, weight_ref, *out_refs):
        for d, out_ref in enumerate(out_refs):

            @pl.when(pl.program_id(0) == d)
            def _():
                total = 0.0
                for q in range(quarters):
                    rows = jnp.concatenate(
                        [ref[0, q, m, 0] for ref in (near_ref, other_ref) for m in range(batches)]
                    )
                    total += dot(rows, weight_ref[q], (1, 1))
                out_ref[...] = total.astype(BF16).reshape(shape)

    def place(d, y):
        source = (y[0] + d) & 3
        return (source >> 1, 0, 0, source & 1, 0, 0)

    piece = pl.BlockSpec((1, quarters, batches, 1, part, ff), place)
    return call(
        body,
        (4,),
        [piece, piece, pl.BlockSpec(weight.shape, lambda d, y: (0, 0, 0))],
        [pl.BlockSpec(shape, lambda d, y: (0, 0, 0, 0))] * 4,
        [jax.ShapeDtypeStruct(shape, BF16)] * 4,
        1,
        16 * batches * part * quarters * ff * width,
    )(here, near, other, weight)


def combine(half, first, returned, table, far, shape, so_far):
    returned = [returned[d] for d in (0, 3, 2, 1)]
    _, batches, part, width = returned[0].shape
    rows, tok = 4 * part, shape[3]

    def body(zh_ref, *refs):
        out_ref, table_ref = refs[-1], refs[4]
        seat = table_ref[0, 0:1, :].astype(I32)
        hit = seat == lax.broadcasted_iota(I32, (8 * tok, rows), 0)
        gate = jnp.where(hit, table_ref[0, 1:2, :], 0.0)
        high = gate.astype(BF16)
        low = (gate - high.astype(F32)).astype(BF16)
        source = jnp.concatenate([ref[0, 0] for ref in refs[:4]], axis=0)
        total = dot(high, source, (1, 0)) + dot(low, source, (1, 0))
        out_ref[...] = total.astype(BF16).reshape(out_ref.shape)

    extra = () if so_far is None else (so_far,)
    return call(
        body,
        (2, batches),
        [pl.BlockSpec((1, 1, part, width), lambda k, m, zh: (k, m, 0, 0))] * 4
        + [pl.BlockSpec((1, 2, rows), lambda k, m, zh: (half * 4 + k * 2 + m + first, 0, 0))]
        + [pl.BlockSpec(memory_space=pl.ANY)] * len(extra),
        pl.BlockSpec((1, 8, 1, tok, width), lambda k, m, zh: (zh[0] ^ half, 0, m + first, 0, k)),
        jax.ShapeDtypeStruct(shape, BF16),
        1,
        8 * batches * rows * 8 * tok * width,
        aliases={6: 0} if extra else {},
    )(far, *returned, table, *extra)


def weight_sum(first, inbound, near, other, here, so_far, scale, kind):
    _, quarters, batches, _, part, ff = near.shape
    width = inbound[0].shape[3]

    def body(y_ref, *refs):
        near_ref, other_ref = refs[4:6]
        out_ref, total = refs[-2:]

        @pl.when(pl.program_id(0) == 0)
        def _():
            total[...] = jnp.zeros_like(total) if so_far is None else refs[6][...]

        for d in range(4):

            @pl.when(pl.program_id(0) == d)
            def _():
                source = refs[d][...].reshape(2 * batches * part, width)
                for q in range(quarters):
                    rows = jnp.concatenate(
                        [ref[0, q, m, 0] for ref in (near_ref, other_ref) for m in range(batches)]
                    )
                    total[q] += dot(source, rows, (0, 0))

        @pl.when(pl.program_id(0) == 3)
        def _():
            out_ref[...] = (total[...] * scale).astype(kind)

    def place(d, y):
        source = (y[0] - d) & 3
        return (source >> 1, 0, 0, source & 1, 0, 0)

    piece = pl.BlockSpec((1, quarters, batches, 1, part, ff), place)
    whole = pl.BlockSpec((quarters, width, ff), lambda d, y: (0, 0, 0))
    extra = () if so_far is None else (so_far,)
    return call(
        body,
        (4,),
        [pl.BlockSpec((2, batches, part, width), lambda d, y: (0, first, 0, 0))] * 4
        + [piece, piece]
        + [whole] * len(extra),
        whole,
        jax.ShapeDtypeStruct((quarters, width, ff), kind),
        1,
        16 * batches * part * width * quarters * ff,
        scratch=(pltpu.VMEM((quarters, width, ff), F32),),
    )(here, *inbound, near, other, *extra)


def slot_tables(expert_ids, slot_index, gate_weights, capacity, places):
    rows = expert_ids.shape[1]
    position = jnp.where(slot_index >= 0, expert_ids * capacity + slot_index, -1)
    matches = position[..., None] == jnp.arange(places, dtype=I32)
    token = jnp.arange(1, rows + 1, dtype=F32)[None, :, None, None]
    held = jnp.sum(jnp.where(matches, token, 0.0), axis=(1, 2)) - 1.0
    gate = jnp.sum(jnp.where(matches, gate_weights[..., None], 0.0), axis=(1, 2))
    return held, gate


def by(flag, a, b):
    return jnp.where(flag == 0, a, b), jnp.where(flag == 0, b, a)


def on_device(
    tokens,
    expert_ids,
    slot_index,
    gate_weights,
    up_gradient,
    up_weight,
    attention_partial,
    residual_gradient,
):
    nzl, ny, nx = (lax.axis_size(a) for a in ("zl", "y", "x"))
    zh, co, x = (lax.axis_index(a) for a in ("zh", "co", "x"))
    batches, tok, width = tokens.shape
    quarter, eighth = width // nx, width // nx // 2
    buffer_rows, ff = up_gradient.shape[3:]
    capacity = buffer_rows // (nzl * ny)
    rows = batches * buffer_rows
    far = zh.astype(I32).reshape(1)
    y = lax.axis_index("y")
    here = y.astype(I32).reshape(1)

    part = nzl * capacity

    def gather(v):
        v = lax.all_to_all(
            jnp.broadcast_to(v, (nx,) + v.shape), "x", split_axis=0, concat_axis=0, tiled=True
        )
        return v.reshape(2, 2, -1, 2, part, ff)

    def along_y(parts):
        return [
            v if d == 0 else lax.ppermute(v, "y", [(i, (i + d) % ny) for i in range(ny)])
            for d, v in enumerate(parts)
        ]

    r = jnp.arange(rows, dtype=I32)
    source_row = (
        ((r // (part * ny)) * nzl + (r // capacity) % nzl) * ny + (r // part) % ny
    ) * capacity + r % capacity
    order = (source_row[:, None] == r[None, :]).astype(BF16)
    hidden = dot(order, up_gradient.reshape(rows, ff), (1, 0)).astype(BF16)
    halves = hidden.reshape(batches, 2, 2 * part, ff)
    xh = x // 2
    keep, send = by(xh, halves[:, 0], halves[:, 1])
    taken = lax.ppermute(send, "x", [(i, (i + 2) % nx) for i in range(nx)])
    stay, leave = by(xh ^ zh, keep, taken)
    near = gather(stay)

    expert_ids, slot_index, gate_weights, send = lax.optimization_barrier(
        (expert_ids, slot_index, gate_weights, send)
    )
    held, gate = slot_tables(expert_ids, slot_index, gate_weights, capacity, nzl * ny * capacity)
    high = lax.reduce_precision(gate, 8, 7)
    middle = lax.reduce_precision(gate - high, 8, 7)
    table = jnp.stack([held, high, middle, gate - high - middle])
    table = table.reshape(4, batches, nzl, 2, 2 * capacity).transpose(2, 0, 1, 3, 4)
    table = table.reshape(batches * tok, 2 * capacity).astype(BF16)
    table = jnp.pad(table, ((0, 0), (0, 64 - 2 * capacity)))

    own_part = lax.dynamic_slice_in_dim(tokens, x * quarter, quarter, 2)
    own_part = own_part.reshape(batches * tok, 2, eighth)
    mine, theirs = by(co, own_part[:, 0], own_part[:, 1])
    theirs = lax.ppermute(jnp.concatenate([theirs, table], axis=1), "co", SWAP)
    line = jnp.concatenate([mine, theirs[:, :eighth], table, theirs[:, eighth:]], axis=1)
    line = lax.all_gather(line, ("zh", "zl"), axis=0, tiled=True)

    cut = up_weight.reshape(2, eighth, ff)
    mine, theirs = by(co, cut[0], cut[1])
    weight = jnp.stack(by(co, mine, lax.ppermute(theirs, "co", SWAP)))

    near_other = lax.ppermute(near, "co", SWAP)
    back = rows_back(near, near_other, weight, here)
    wide, wide_other, wide_back = [], [], []
    for m in range(batches):
        crossed = lax.ppermute(leave[m], "zh", SWAP)
        if m + 1 < batches:
            crossed, leave = lax.optimization_barrier((crossed, leave))
        wide.append(gather(crossed))
        if m == 0:
            wide[0], back = lax.optimization_barrier((wide[0], back))
        wide_other.append(lax.ppermute(wide[m], "co", SWAP))
        wide_back.append(rows_back(wide[m], wide_other[m], weight, here))

    column = lax.dynamic_slice(
        line.reshape(2 * nzl, batches * tok, -1),
        (0, lax.axis_index("zl") * 16, quarter),
        (2 * nzl, 16, 128),
    ).reshape(2, nzl, 4, batches, 2, 2, 64)[..., : 2 * capacity]
    column = jnp.where(zh == 0, column, column[::-1]).astype(F32)
    column = column.reshape(2, nzl, 4, batches, 2, 2, 2, capacity)
    column = column.transpose(2, 0, 5, 3, 4, 6, 1, 7).reshape(
        4, 4 * batches, ny, nzl, capacity
    )
    column = lax.dynamic_slice_in_dim(jnp.concatenate([column, column], axis=2), y, ny, 2)
    start = jnp.arange(nzl, dtype=F32)[:, None] * tok
    seats = jnp.where(column[0] >= 0, column[0] + start, -1.0)
    column = jnp.stack([seats, column[1] + (column[2] + column[3])])
    column = column.reshape(2, 4 * batches, buffer_rows)
    lying, standing = column.transpose(1, 0, 2), column.transpose(1, 2, 0)

    shape = (2, nzl, batches, tok, quarter)
    spread = combine(0, 0, along_y(back), lying, far, shape, None)
    for m in range(batches):
        spread = combine(1, m, along_y(wide_back[m]), lying, far, shape, spread)
    expert_part = lax.psum_scatter(
        spread.reshape(2 * nzl * batches * tok, quarter),
        ("zh", "zl"),
        scatter_dimension=0,
        tiled=True,
    )

    line = line.reshape(2 * nzl, batches, tok, -1)
    line, attention_partial, last = lax.optimization_barrier(
        (line, attention_partial, wide_back[-1])
    )
    inbound = along_y(pick_rows(0, line, standing, far, eighth))
    line, _ = lax.optimization_barrier((line, spread))
    inbound_far = along_y(pick_rows(1, line, standing, far, eighth))
    total = weight_sum(0, inbound, near, near_other, here, None, 1.0, F32)
    for m in range(batches):
        last = m + 1 == batches
        total = weight_sum(
            m,
            inbound_far,
            wide[m],
            wide_other[m],
            here,
            total,
            1.0 / (2 * SIZES[1]) if last else 1.0,
            BF16 if last else F32,
        )
    mine, theirs = by(co, total[0], total[1])
    weight_gradient = jnp.concatenate(by(co, mine, lax.ppermute(theirs, "co", SWAP)))

    shares = attention_partial.reshape(batches * tok, nx, quarter).transpose(1, 0, 2)
    shares = lax.all_to_all(shares, "x", split_axis=0, concat_axis=0, tiled=True)
    base = residual_gradient.reshape(batches * tok, quarter).astype(F32) + jnp.sum(
        shares.astype(F32), axis=0
    )
    other = lax.ppermute(expert_part[:, eighth:], "co", SWAP)
    expert_part = jnp.concatenate(by(co, expert_part[:, :eighth], other), axis=1)
    token_gradient = (base + expert_part.astype(F32)).astype(BF16)
    return (token_gradient.reshape(batches, tok, quarter), weight_gradient[None])


def solution(mesh):
    split = Mesh(mesh.devices.reshape(SIZES), AXES)
    dp, ep, tp = ("zh", "co"), ("zl", "y"), "x"
    return jax.shard_map(
        on_device,
        mesh=split,
        in_specs=(
            P(None, dp + ep, None),
            P(None, dp + ep, None),
            P(None, dp + ep, None),
            P(None, dp + ep, None),
            P(dp, None, ep, None, tp),
            P(ep, tp, dp),
            P(tp, None, dp + ep, None),
            P(None, dp + ep, tp),
        ),
        out_specs=(P(None, dp + ep, tp), P(ep, tp, dp)),
        check_vma=False,
    )
```

```python
import jax
import jax.numpy as jnp
from jax import lax
from jax.experimental import pallas as pl
from jax.experimental.pallas import tpu as pltpu
from jax.sharding import Mesh, PartitionSpec as P

AXES = ("zh", "co", "zl", "y", "x")
SIZES = (2, 2, 8, 4, 4)
SWAP = [(0, 1), (1, 0)]
BF16, F32, I32 = jnp.bfloat16, jnp.float32, jnp.int32
VMEM = 48 * 1024 * 1024


def dot(a, b, over):
    return lax.dot_general(a, b, ((over[:1], over[1:]), ((), ())), preferred_element_type=F32)


def call(body, grid, in_specs, out_spec, out_shape, prefetch, flops, scratch=(), aliases={}):
    return pl.pallas_call(
        body,
        grid_spec=pltpu.PrefetchScalarGridSpec(
            num_scalar_prefetch=prefetch,
            grid=grid,
            in_specs=in_specs,
            out_specs=out_spec,
            scratch_shapes=scratch,
        ),
        out_shape=out_shape,
        input_output_aliases=aliases,
        compiler_params=pltpu.CompilerParams(vmem_limit_bytes=VMEM),
        cost_estimate=pl.CostEstimate(flops=flops, bytes_accessed=1 << 23, transcendentals=0),
    )


def pick_rows(half, line, table, far, width):
    batches, tok = line.shape[1:3]
    rows = table.shape[1]
    part = rows // SIZES[3]

    def body(zh_ref, line_ref, table_ref, out_ref):
        source = line_ref[...].reshape(8 * tok, width)
        seat = table_ref[0, :, 0:1].astype(I32)
        hit = seat == lax.broadcasted_iota(I32, (rows, 8 * tok), 1)
        taken = dot(jnp.where(hit, 1.0, 0.0).astype(BF16), source, (1, 0))
        taken = (taken * table_ref[0, :, 1:2]).astype(BF16)
        out_ref[...] = taken.reshape(out_ref.shape)

    return call(
        body,
        (2, batches),
        [
            pl.BlockSpec((8, 1, tok, width), lambda k, m, zh: (zh[0] ^ half, m, 0, k)),
            pl.BlockSpec((1, rows, 2), lambda k, m, zh: (half * 4 + k * 2 + m, 0, 0)),
        ],
        pl.BlockSpec((4, 1, 1, part, width), lambda k, m, zh: (0, k, m, 0, 0)),
        jax.ShapeDtypeStruct((4, 2, batches, part, width), BF16),
        1,
        8 * rows * 8 * tok * width,
    )(far, line, table)


def rows_back(near, other, weight):
    pairs, quarters, rows, ff = near.shape
    width = weight.shape[1]
    part = rows // 2

    def body(near_ref, other_ref, weight_ref, out_ref):
        for k, ref in enumerate((near_ref, other_ref)):
            total = dot(ref[0, 0], weight_ref[0], (1, 1)) + dot(ref[0, 1], weight_ref[1], (1, 1))
            total = total.astype(BF16)
            out_ref[0, k] = total[:part]
            out_ref[1, k] = total[part:]

    piece = pl.BlockSpec((1, quarters, rows, ff), lambda h: (h, 0, 0, 0))
    return call(
        body,
        (pairs,),
        [piece, piece, pl.BlockSpec(weight.shape, lambda h: (0, 0, 0))],
        pl.BlockSpec((2, 2, part, width), lambda h: (h, 0, 0, 0)),
        jax.ShapeDtypeStruct((4, 2, part, width), BF16),
        0,
        8 * pairs * rows * ff * width,
    )(near, other, weight)


def combine(half, returned, table, far, tok, so_far):
    _, _, batches, part, width = returned.shape
    rows = 4 * part

    def body(zh_ref, back_ref, table_ref, *refs):
        out_ref = refs[-1]
        seat = table_ref[0, 0:1, :].astype(I32)
        hit = seat == lax.broadcasted_iota(I32, (8 * tok, rows), 0)
        gate = jnp.where(hit, table_ref[0, 1:2, :], 0.0)
        high = gate.astype(BF16)
        low = (gate - high.astype(F32)).astype(BF16)
        source = back_ref[...].reshape(rows, width)
        total = dot(high, source, (1, 0)) + dot(low, source, (1, 0))
        out_ref[...] = total.astype(BF16).reshape(out_ref.shape)

    extra = () if so_far is None else (so_far,)
    return call(
        body,
        (2, batches),
        [
            pl.BlockSpec((4, 1, 1, part, width), lambda k, m, zh: (0, k, m, 0, 0)),
            pl.BlockSpec((1, 2, rows), lambda k, m, zh: (half * 4 + k * 2 + m, 0, 0)),
        ]
        + [pl.BlockSpec(memory_space=pl.ANY)] * len(extra),
        pl.BlockSpec((1, 8, 1, tok, width), lambda k, m, zh: (zh[0] ^ half, 0, m, 0, k)),
        jax.ShapeDtypeStruct((2, 8, batches, tok, 2 * width), BF16),
        1,
        16 * rows * 8 * tok * width,
        aliases={3: 0} if extra else {},
    )(far, returned, table, *extra)


def weight_sum(inbound, near, other, so_far, scale, kind):
    count, _, part, width = inbound.shape
    quarters, ff = near.shape[1], near.shape[3]

    def body(in_ref, near_ref, other_ref, *refs):
        out_ref, total = refs[-2:]

        @pl.when(pl.program_id(0) == 0)
        def _():
            total[...] = jnp.zeros_like(total) if so_far is None else refs[0][...]

        for q in range(quarters):
            total[q] += dot(in_ref[0, 0], near_ref[0, q], (0, 0)) + dot(
                in_ref[0, 1], other_ref[0, q], (0, 0)
            )

        @pl.when(pl.program_id(0) == count - 1)
        def _():
            out_ref[...] = (total[...] * scale).astype(kind)

    piece = pl.BlockSpec((1, quarters, part, ff), lambda y: (y // 2, 0, y % 2, 0))
    whole = pl.BlockSpec((quarters, width, ff), lambda y: (0, 0, 0))
    extra = () if so_far is None else (so_far,)
    return call(
        body,
        (count,),
        [pl.BlockSpec((1, 2, part, width), lambda y: (y, 0, 0, 0)), piece, piece]
        + [whole] * len(extra),
        whole,
        jax.ShapeDtypeStruct((quarters, width, ff), kind),
        0,
        4 * count * part * width * quarters * ff,
        (pltpu.VMEM((quarters, width, ff), F32),),
    )(inbound, near, other, *extra)


def slot_tables(expert_ids, slot_index, gate_weights, capacity, places):
    rows = expert_ids.shape[1]
    position = jnp.where(slot_index >= 0, expert_ids * capacity + slot_index, -1)
    matches = position[..., None] == jnp.arange(places, dtype=I32)
    token = jnp.arange(1, rows + 1, dtype=F32)[None, :, None, None]
    held = jnp.sum(jnp.where(matches, token, 0.0), axis=(1, 2)) - 1.0
    gate = jnp.sum(jnp.where(matches, gate_weights[..., None], 0.0), axis=(1, 2))
    return held, gate


def by(flag, a, b):
    return jnp.where(flag == 0, a, b), jnp.where(flag == 0, b, a)


def on_device(
    tokens,
    expert_ids,
    slot_index,
    gate_weights,
    up_gradient,
    up_weight,
    attention_partial,
    residual_gradient,
):
    nzl, ny, nx = (lax.axis_size(a) for a in ("zl", "y", "x"))
    zh, co, x = (lax.axis_index(a) for a in ("zh", "co", "x"))
    batches, tok, width = tokens.shape
    quarter, eighth = width // nx, width // nx // 2
    buffer_rows, ff = up_gradient.shape[3:]
    capacity = buffer_rows // (nzl * ny)
    rows = batches * buffer_rows
    far = zh.astype(I32).reshape(1)

    def gather(v):
        return lax.all_to_all(
            jnp.broadcast_to(v, (nx,) + v.shape), "x", split_axis=0, concat_axis=0, tiled=True
        ).reshape((2, 2) + v.shape)

    def along_y(v):
        shape = v.shape
        v = v.reshape(ny, -1, shape[-1])
        return lax.all_to_all(v, "y", split_axis=0, concat_axis=0, tiled=True).reshape(shape)

    cut = up_weight.reshape(2, eighth, ff)
    mine, theirs = by(co, cut[0], cut[1])
    weight = jnp.stack(by(co, mine, lax.ppermute(theirs, "co", SWAP)))

    r = jnp.arange(rows, dtype=I32)
    r_batch = (r // (capacity * nzl)) % batches
    source_row = (
        (r_batch * nzl + (r // capacity) % nzl) * ny + r // (capacity * nzl * batches)
    ) * capacity + r % capacity
    order = (source_row[:, None] == r[None, :]).astype(BF16)
    hidden = dot(order, up_gradient.reshape(rows, ff), (1, 0)).astype(BF16)
    halves = hidden.reshape(2, rows // 2, ff)
    xh = x // 2
    keep, send = by(xh, halves[0], halves[1])
    taken = lax.ppermute(send, "x", [(i, (i + 2) % nx) for i in range(nx)])
    stay, leave = by(xh ^ zh, keep, taken)
    stay, weight = lax.optimization_barrier((stay, weight))
    crossed = lax.ppermute(leave, "zh", SWAP)
    near = gather(stay)

    expert_ids, slot_index, gate_weights, send = lax.optimization_barrier(
        (expert_ids, slot_index, gate_weights, send)
    )
    held, gate = slot_tables(expert_ids, slot_index, gate_weights, capacity, nzl * ny * capacity)
    high = lax.reduce_precision(gate, 8, 7)
    middle = lax.reduce_precision(gate - high, 8, 7)
    table = jnp.stack([held, high, middle, gate - high - middle])
    table = table.reshape(4, batches, nzl, 2, 2 * capacity).transpose(2, 0, 1, 3, 4)
    table = table.reshape(batches * tok, 2 * capacity).astype(BF16)
    table = jnp.pad(table, ((0, 0), (0, 64 - 2 * capacity)))

    own_part = lax.dynamic_slice_in_dim(tokens, x * quarter, quarter, 2)
    own_part = own_part.reshape(batches * tok, 2, eighth)
    mine, theirs = by(co, own_part[:, 0], own_part[:, 1])
    theirs = lax.ppermute(jnp.concatenate([theirs, table], axis=1), "co", SWAP)
    line = jnp.concatenate([mine, theirs[:, :eighth], table, theirs[:, eighth:]], axis=1)
    line, near = lax.optimization_barrier((line, near))
    line = lax.all_gather(line, ("zh", "zl"), axis=0, tiled=True)

    near_other = lax.ppermute(near, "co", SWAP)
    back = rows_back(near, near_other, weight)
    wide = gather(crossed)
    wide, back = lax.optimization_barrier((wide, back))
    back = along_y(back)
    wide_other = lax.ppermute(wide, "co", SWAP)
    wide_back = rows_back(wide, wide_other, weight)
    wide_back, back = lax.optimization_barrier((wide_back, back))
    wide_back = along_y(wide_back)

    column = lax.dynamic_slice(
        line.reshape(2 * nzl, batches * tok, -1),
        (0, lax.axis_index("zl") * 16, quarter),
        (2 * nzl, 16, 128),
    ).reshape(2, nzl, 4, batches, 2, 2, 64)[..., : 2 * capacity]
    column = jnp.where(zh == 0, column, column[::-1]).astype(F32)
    column = column.reshape(2, nzl, 4, batches, 2, 2, 2, capacity)
    column = column.transpose(2, 0, 5, 3, 4, 6, 1, 7)
    start = jnp.arange(nzl, dtype=F32)[:, None] * tok
    seats = jnp.where(column[0] >= 0, column[0] + start, -1.0)
    column = jnp.stack([seats, column[1] + (column[2] + column[3])])
    column = column.reshape(2, 4 * batches, buffer_rows)
    lying, standing = column.transpose(1, 0, 2), column.transpose(1, 2, 0)

    split = (4, 2, batches, nzl * capacity, eighth)
    spread = combine(0, back.reshape(split), lying, far, tok, None)
    spread = combine(1, wide_back.reshape(split), lying, far, tok, spread)
    expert_part = lax.psum_scatter(
        spread.reshape(2 * nzl * batches * tok, quarter),
        ("zh", "zl"),
        scatter_dimension=0,
        tiled=True,
    )

    line = line.reshape(2 * nzl, batches, tok, -1)
    line, wide_back = lax.optimization_barrier((line, wide_back))
    inbound = along_y(pick_rows(0, line, standing, far, eighth))
    line, inbound, attention_partial = lax.optimization_barrier(
        (line, inbound, attention_partial)
    )
    inbound_far = along_y(pick_rows(1, line, standing, far, eighth))
    split = (4, 2, batches * nzl * capacity, eighth)
    total = weight_sum(inbound.reshape(split), near, near_other, None, 1.0, F32)
    total = weight_sum(
        inbound_far.reshape(split), wide, wide_other, total, 1.0 / (2 * SIZES[1]), BF16
    )
    mine, theirs = by(co, total[0], total[1])
    weight_gradient = jnp.concatenate(by(co, mine, lax.ppermute(theirs, "co", SWAP)))

    shares = attention_partial.reshape(batches * tok, nx, quarter).transpose(1, 0, 2)
    shares = lax.all_to_all(shares, "x", split_axis=0, concat_axis=0, tiled=True)
    base = residual_gradient.reshape(batches * tok, quarter).astype(F32) + jnp.sum(
        shares.astype(F32), axis=0
    )
    other = lax.ppermute(expert_part[:, eighth:], "co", SWAP)
    expert_part = jnp.concatenate(by(co, expert_part[:, :eighth], other), axis=1)
    token_gradient = (base + expert_part.astype(F32)).astype(BF16)
    return (token_gradient.reshape(batches, tok, quarter), weight_gradient[None])


def solution(mesh):
    split = Mesh(mesh.devices.reshape(SIZES), AXES)
    dp, ep, tp = ("zh", "co"), ("zl", "y"), "x"
    return jax.shard_map(
        on_device,
        mesh=split,
        in_specs=(
            P(None, dp + ep, None),
            P(None, dp + ep, None),
            P(None, dp + ep, None),
            P(None, dp + ep, None),
            P(dp, None, ep, None, tp),
            P(ep, tp, dp),
            P(tp, None, dp + ep, None),
            P(None, dp + ep, tp),
        ),
        out_specs=(P(None, dp + ep, tp), P(ep, tp, dp)),
        check_vma=False,
    )
```

```python
import jax
import jax.numpy as jnp
from jax import lax
from jax.experimental import pallas as pl
from jax.experimental.pallas import tpu as pltpu
from jax.sharding import Mesh, PartitionSpec as P

AXES = ("zh", "co", "zl", "y", "x")
SIZES = (2, 2, 8, 4, 4)
SWAP = [(0, 1), (1, 0)]
BF16, F32, I32 = jnp.bfloat16, jnp.float32, jnp.int32
VMEM = 48 * 1024 * 1024


def dot(a, b, over):
    return lax.dot_general(a, b, ((over[:1], over[1:]), ((), ())), preferred_element_type=F32)


def call(body, grid, in_specs, out_spec, out_shape, prefetch, flops, scratch=(), aliases={}):
    return pl.pallas_call(
        body,
        grid_spec=pltpu.PrefetchScalarGridSpec(
            num_scalar_prefetch=prefetch,
            grid=grid,
            in_specs=in_specs,
            out_specs=out_spec,
            scratch_shapes=scratch,
        ),
        out_shape=out_shape,
        input_output_aliases=aliases,
        compiler_params=pltpu.CompilerParams(vmem_limit_bytes=VMEM),
        cost_estimate=pl.CostEstimate(flops=flops, bytes_accessed=1 << 23, transcendentals=0),
    )


def pick_rows(half, line, table, far, width):
    batches, tok = line.shape[1:3]
    rows = table.shape[1]
    part = rows // 4

    def body(zh_ref, line_ref, table_ref, *out_refs):
        source = line_ref[...].reshape(8 * tok, width)
        seat = table_ref[0, :, 0:1].astype(I32)
        hit = seat == lax.broadcasted_iota(I32, (rows, 8 * tok), 1)
        taken = dot(jnp.where(hit, 1.0, 0.0).astype(BF16), source, (1, 0))
        taken = (taken * table_ref[0, :, 1:2]).astype(BF16)
        for d, ref in enumerate(out_refs):
            ref[0, 0] = taken[d * part : (d + 1) * part]

    return call(
        body,
        (2, batches),
        [
            pl.BlockSpec((8, 1, tok, width), lambda k, m, zh: (zh[0] ^ half, m, 0, k)),
            pl.BlockSpec((1, rows, 2), lambda k, m, zh: (half * 4 + k * 2 + m, 0, 0)),
        ],
        [pl.BlockSpec((1, 1, part, width), lambda k, m, zh: (k, m, 0, 0))] * 4,
        [jax.ShapeDtypeStruct((2, batches, part, width), BF16)] * 4,
        1,
        8 * rows * 8 * tok * width,
    )(far, line, table)


def rows_back(near, other, weight, here):
    _, quarters, rows, ff = near.shape
    width = weight.shape[1]
    part = rows // 2

    def body(y_ref, near_ref, other_ref, weight_ref, *out_refs):
        for d, out_ref in enumerate(out_refs):

            @pl.when(pl.program_id(0) == d)
            def _():
                for k, ref in enumerate((near_ref, other_ref)):
                    total = dot(ref[0, 0], weight_ref[0], (1, 1))
                    total += dot(ref[0, 1], weight_ref[1], (1, 1))
                    out_ref[k] = total.astype(BF16)

    def place(d, y):
        source = (y[0] + d) & 3
        return (source >> 1, 0, source & 1, 0)

    piece = pl.BlockSpec((1, quarters, part, ff), place)
    return call(
        body,
        (4,),
        [piece, piece, pl.BlockSpec(weight.shape, lambda d, y: (0, 0, 0))],
        [pl.BlockSpec((2, part, width), lambda d, y: (0, 0, 0))] * 4,
        [jax.ShapeDtypeStruct((2, part, width), BF16)] * 4,
        1,
        16 * part * quarters * ff * width,
    )(here, near, other, weight)


def combine(half, returned, table, far, tok, so_far):
    returned = [returned[d] for d in (0, 3, 2, 1)]
    _, batches, part, width = returned[0].shape
    rows = 4 * part

    def body(zh_ref, *refs):
        out_ref, table_ref = refs[-1], refs[4]
        seat = table_ref[0, 0:1, :].astype(I32)
        hit = seat == lax.broadcasted_iota(I32, (8 * tok, rows), 0)
        gate = jnp.where(hit, table_ref[0, 1:2, :], 0.0)
        high = gate.astype(BF16)
        low = (gate - high.astype(F32)).astype(BF16)
        source = jnp.concatenate([ref[0, 0] for ref in refs[:4]], axis=0)
        total = dot(high, source, (1, 0)) + dot(low, source, (1, 0))
        out_ref[...] = total.astype(BF16).reshape(out_ref.shape)

    extra = () if so_far is None else (so_far,)
    return call(
        body,
        (2, batches),
        [pl.BlockSpec((1, 1, part, width), lambda k, m, zh: (k, m, 0, 0))] * 4
        + [pl.BlockSpec((1, 2, rows), lambda k, m, zh: (half * 4 + k * 2 + m, 0, 0))]
        + [pl.BlockSpec(memory_space=pl.ANY)] * len(extra),
        pl.BlockSpec((1, 8, 1, tok, width), lambda k, m, zh: (zh[0] ^ half, 0, m, 0, k)),
        jax.ShapeDtypeStruct((2, 8, batches, tok, 2 * width), BF16),
        1,
        16 * rows * 8 * tok * width,
        aliases={6: 0} if extra else {},
    )(far, *returned, table, *extra)


def weight_sum(inbound, near, other, here, so_far, scale, kind):
    _, part, width = inbound[0].shape
    quarters, ff = near.shape[1], near.shape[3]

    def body(y_ref, *refs):
        near_ref, other_ref = refs[4:6]
        out_ref, total = refs[-2:]

        @pl.when(pl.program_id(0) == 0)
        def _():
            total[...] = jnp.zeros_like(total) if so_far is None else refs[6][...]

        for d in range(4):

            @pl.when(pl.program_id(0) == d)
            def _():
                for q in range(quarters):
                    total[q] += dot(refs[d][0], near_ref[0, q], (0, 0)) + dot(
                        refs[d][1], other_ref[0, q], (0, 0)
                    )

        @pl.when(pl.program_id(0) == 3)
        def _():
            out_ref[...] = (total[...] * scale).astype(kind)

    def place(d, y):
        source = (y[0] - d) & 3
        return (source >> 1, 0, source & 1, 0)

    piece = pl.BlockSpec((1, quarters, part, ff), place)
    whole = pl.BlockSpec((quarters, width, ff), lambda d, y: (0, 0, 0))
    extra = () if so_far is None else (so_far,)
    return call(
        body,
        (4,),
        [pl.BlockSpec((2, part, width), lambda d, y: (0, 0, 0))] * 4
        + [piece, piece]
        + [whole] * len(extra),
        whole,
        jax.ShapeDtypeStruct((quarters, width, ff), kind),
        1,
        16 * part * width * quarters * ff,
        scratch=(pltpu.VMEM((quarters, width, ff), F32),),
    )(here, *inbound, near, other, *extra)


def slot_tables(expert_ids, slot_index, gate_weights, capacity, places):
    rows = expert_ids.shape[1]
    position = jnp.where(slot_index >= 0, expert_ids * capacity + slot_index, -1)
    matches = position[..., None] == jnp.arange(places, dtype=I32)
    token = jnp.arange(1, rows + 1, dtype=F32)[None, :, None, None]
    held = jnp.sum(jnp.where(matches, token, 0.0), axis=(1, 2)) - 1.0
    gate = jnp.sum(jnp.where(matches, gate_weights[..., None], 0.0), axis=(1, 2))
    return held, gate


def by(flag, a, b):
    return jnp.where(flag == 0, a, b), jnp.where(flag == 0, b, a)


def on_device(
    tokens,
    expert_ids,
    slot_index,
    gate_weights,
    up_gradient,
    up_weight,
    attention_partial,
    residual_gradient,
):
    nzl, ny, nx = (lax.axis_size(a) for a in ("zl", "y", "x"))
    zh, co, x = (lax.axis_index(a) for a in ("zh", "co", "x"))
    batches, tok, width = tokens.shape
    quarter, eighth = width // nx, width // nx // 2
    buffer_rows, ff = up_gradient.shape[3:]
    capacity = buffer_rows // (nzl * ny)
    rows = batches * buffer_rows
    far = zh.astype(I32).reshape(1)
    y = lax.axis_index("y")
    here = y.astype(I32).reshape(1)

    def gather(v):
        return lax.all_to_all(
            jnp.broadcast_to(v, (nx,) + v.shape), "x", split_axis=0, concat_axis=0, tiled=True
        ).reshape((2, 2) + v.shape)

    def along_y(parts, shape):
        moved = [
            v if d == 0 else lax.ppermute(v, "y", [(i, (i + d) % ny) for i in range(ny)])
            for d, v in enumerate(parts)
        ]
        return [v.reshape(shape) for v in moved]

    cut = up_weight.reshape(2, eighth, ff)
    mine, theirs = by(co, cut[0], cut[1])
    weight = jnp.stack(by(co, mine, lax.ppermute(theirs, "co", SWAP)))

    r = jnp.arange(rows, dtype=I32)
    r_batch = (r // (capacity * nzl)) % batches
    source_row = (
        (r_batch * nzl + (r // capacity) % nzl) * ny + r // (capacity * nzl * batches)
    ) * capacity + r % capacity
    order = (source_row[:, None] == r[None, :]).astype(BF16)
    hidden = dot(order, up_gradient.reshape(rows, ff), (1, 0)).astype(BF16)
    halves = hidden.reshape(2, rows // 2, ff)
    xh = x // 2
    keep, send = by(xh, halves[0], halves[1])
    taken = lax.ppermute(send, "x", [(i, (i + 2) % nx) for i in range(nx)])
    stay, leave = by(xh ^ zh, keep, taken)
    crossed = lax.ppermute(leave, "zh", SWAP)
    near = gather(stay)

    expert_ids, slot_index, gate_weights, send = lax.optimization_barrier(
        (expert_ids, slot_index, gate_weights, send)
    )
    held, gate = slot_tables(expert_ids, slot_index, gate_weights, capacity, nzl * ny * capacity)
    high = lax.reduce_precision(gate, 8, 7)
    middle = lax.reduce_precision(gate - high, 8, 7)
    table = jnp.stack([held, high, middle, gate - high - middle])
    table = table.reshape(4, batches, nzl, 2, 2 * capacity).transpose(2, 0, 1, 3, 4)
    table = table.reshape(batches * tok, 2 * capacity).astype(BF16)
    table = jnp.pad(table, ((0, 0), (0, 64 - 2 * capacity)))

    own_part = lax.dynamic_slice_in_dim(tokens, x * quarter, quarter, 2)
    own_part = own_part.reshape(batches * tok, 2, eighth)
    mine, theirs = by(co, own_part[:, 0], own_part[:, 1])
    theirs = lax.ppermute(jnp.concatenate([theirs, table], axis=1), "co", SWAP)
    line = jnp.concatenate([mine, theirs[:, :eighth], table, theirs[:, eighth:]], axis=1)
    line = lax.all_gather(line, ("zh", "zl"), axis=0, tiled=True)

    split = (2, batches, nzl * capacity, eighth)
    near, crossed = lax.optimization_barrier((near, crossed))
    near_other = lax.ppermute(near, "co", SWAP)
    back = rows_back(near, near_other, weight, here)
    wide = gather(crossed)
    wide, back = lax.optimization_barrier((wide, along_y(back, split)))
    wide_other = lax.ppermute(wide, "co", SWAP)
    wide_back = rows_back(wide, wide_other, weight, here)

    column = lax.dynamic_slice(
        line.reshape(2 * nzl, batches * tok, -1),
        (0, lax.axis_index("zl") * 16, quarter),
        (2 * nzl, 16, 128),
    ).reshape(2, nzl, 4, batches, 2, 2, 64)[..., : 2 * capacity]
    column = jnp.where(zh == 0, column, column[::-1]).astype(F32)
    column = column.reshape(2, nzl, 4, batches, 2, 2, 2, capacity)
    column = column.transpose(2, 0, 5, 3, 4, 6, 1, 7).reshape(
        4, 4 * batches, ny, nzl, capacity
    )
    column = lax.dynamic_slice_in_dim(jnp.concatenate([column, column], axis=2), y, ny, 2)
    start = jnp.arange(nzl, dtype=F32)[:, None] * tok
    seats = jnp.where(column[0] >= 0, column[0] + start, -1.0)
    column = jnp.stack([seats, column[1] + (column[2] + column[3])])
    column = column.reshape(2, 4 * batches, buffer_rows)
    lying, standing = column.transpose(1, 0, 2), column.transpose(1, 2, 0)

    spread = combine(0, back, lying, far, tok, None)
    spread = combine(1, along_y(wide_back, split), lying, far, tok, spread)
    expert_part = lax.psum_scatter(
        spread.reshape(2 * nzl * batches * tok, quarter),
        ("zh", "zl"),
        scatter_dimension=0,
        tiled=True,
    )

    line = line.reshape(2 * nzl, batches, tok, -1)
    line, attention_partial, _ = lax.optimization_barrier((line, attention_partial, spread))
    split = (2, batches * nzl * capacity, eighth)
    inbound = along_y(pick_rows(0, line, standing, far, eighth), split)
    inbound_far = along_y(pick_rows(1, line, standing, far, eighth), split)
    total = weight_sum(inbound, near, near_other, here, None, 1.0, F32)
    total = weight_sum(inbound_far, wide, wide_other, here, total, 1.0 / (2 * SIZES[1]), BF16)
    mine, theirs = by(co, total[0], total[1])
    weight_gradient = jnp.concatenate(by(co, mine, lax.ppermute(theirs, "co", SWAP)))

    shares = attention_partial.reshape(batches * tok, nx, quarter).transpose(1, 0, 2)
    shares = lax.all_to_all(shares, "x", split_axis=0, concat_axis=0, tiled=True)
    base = residual_gradient.reshape(batches * tok, quarter).astype(F32) + jnp.sum(
        shares.astype(F32), axis=0
    )
    other = lax.ppermute(expert_part[:, eighth:], "co", SWAP)
    expert_part = jnp.concatenate(by(co, expert_part[:, :eighth], other), axis=1)
    token_gradient = (base + expert_part.astype(F32)).astype(BF16)
    return (token_gradient.reshape(batches, tok, quarter), weight_gradient[None])


def solution(mesh):
    split = Mesh(mesh.devices.reshape(SIZES), AXES)
    dp, ep, tp = ("zh", "co"), ("zl", "y"), "x"
    return jax.shard_map(
        on_device,
        mesh=split,
        in_specs=(
            P(None, dp + ep, None),
            P(None, dp + ep, None),
            P(None, dp + ep, None),
            P(None, dp + ep, None),
            P(dp, None, ep, None, tp),
            P(ep, tp, dp),
            P(tp, None, dp + ep, None),
            P(None, dp + ep, tp),
        ),
        out_specs=(P(None, dp + ep, tp), P(ep, tp, dp)),
        check_vma=False,
    )
```

```python
import jax
import jax.numpy as jnp
from jax import lax
from jax.experimental import pallas as pl
from jax.experimental.pallas import tpu as pltpu
from jax.sharding import Mesh, PartitionSpec as P

AXES = ("zh", "co", "zl", "y", "x")
SIZES = (2, 2, 8, 4, 4)
SWAP = [(0, 1), (1, 0)]
BF16, F32, I32 = jnp.bfloat16, jnp.float32, jnp.int32
VMEM = 48 * 1024 * 1024


def dot(a, b, over):
    return lax.dot_general(a, b, ((over[:1], over[1:]), ((), ())), preferred_element_type=F32)


def call(body, grid, in_specs, out_spec, out_shape, prefetch, flops, scratch=(), aliases={}):
    return pl.pallas_call(
        body,
        grid_spec=pltpu.PrefetchScalarGridSpec(
            num_scalar_prefetch=prefetch,
            grid=grid,
            in_specs=in_specs,
            out_specs=out_spec,
            scratch_shapes=scratch,
        ),
        out_shape=out_shape,
        input_output_aliases=aliases,
        compiler_params=pltpu.CompilerParams(vmem_limit_bytes=VMEM),
        cost_estimate=pl.CostEstimate(flops=flops, bytes_accessed=1 << 23, transcendentals=0),
    )


def pick_rows(half, line, table, far, width):
    batches, tok = line.shape[1:3]
    rows = table.shape[1]
    part = rows // 4

    def body(zh_ref, line_ref, table_ref, *out_refs):
        source = line_ref[...].reshape(8 * tok, width)
        seat = table_ref[0, :, 0:1].astype(I32)
        hit = seat == lax.broadcasted_iota(I32, (rows, 8 * tok), 1)
        taken = dot(jnp.where(hit, 1.0, 0.0).astype(BF16), source, (1, 0))
        taken = (taken * table_ref[0, :, 1:2]).astype(BF16)
        for d, ref in enumerate(out_refs):
            ref[0, 0] = taken[d * part : (d + 1) * part]

    return call(
        body,
        (2, batches),
        [
            pl.BlockSpec((8, 1, tok, width), lambda k, m, zh: (zh[0] ^ half, m, 0, k)),
            pl.BlockSpec((1, rows, 2), lambda k, m, zh: (half * 4 + k * 2 + m, 0, 0)),
        ],
        [pl.BlockSpec((1, 1, part, width), lambda k, m, zh: (k, m, 0, 0))] * 4,
        [jax.ShapeDtypeStruct((2, batches, part, width), BF16)] * 4,
        1,
        8 * rows * 8 * tok * width,
    )(far, line, table)


def rows_back(near, other, weight, here):
    _, quarters, rows, ff = near.shape
    width = weight.shape[1]
    part = rows // 2

    def body(y_ref, near_ref, other_ref, weight_ref, *out_refs):
        for d, out_ref in enumerate(out_refs):

            @pl.when(pl.program_id(0) == d)
            def _():
                for k, ref in enumerate((near_ref, other_ref)):
                    total = dot(ref[0, 0], weight_ref[0], (1, 1))
                    total += dot(ref[0, 1], weight_ref[1], (1, 1))
                    out_ref[k] = total.astype(BF16)

    def place(d, y):
        source = (y[0] + d) & 3
        return (source >> 1, 0, source & 1, 0)

    piece = pl.BlockSpec((1, quarters, part, ff), place)
    return call(
        body,
        (4,),
        [piece, piece, pl.BlockSpec(weight.shape, lambda d, y: (0, 0, 0))],
        [pl.BlockSpec((2, part, width), lambda d, y: (0, 0, 0))] * 4,
        [jax.ShapeDtypeStruct((2, part, width), BF16)] * 4,
        1,
        16 * part * quarters * ff * width,
    )(here, near, other, weight)


def combine(half, returned, table, far, tok, so_far):
    returned = [returned[d] for d in (0, 3, 2, 1)]
    _, batches, part, width = returned[0].shape
    rows = 4 * part

    def body(zh_ref, *refs):
        out_ref, table_ref = refs[-1], refs[4]
        seat = table_ref[0, 0:1, :].astype(I32)
        hit = seat == lax.broadcasted_iota(I32, (8 * tok, rows), 0)
        gate = jnp.where(hit, table_ref[0, 1:2, :], 0.0)
        high = gate.astype(BF16)
        low = (gate - high.astype(F32)).astype(BF16)
        source = jnp.concatenate([ref[0, 0] for ref in refs[:4]], axis=0)
        total = dot(high, source, (1, 0)) + dot(low, source, (1, 0))
        out_ref[...] = total.astype(BF16).reshape(out_ref.shape)

    extra = () if so_far is None else (so_far,)
    return call(
        body,
        (2, batches),
        [pl.BlockSpec((1, 1, part, width), lambda k, m, zh: (k, m, 0, 0))] * 4
        + [pl.BlockSpec((1, 2, rows), lambda k, m, zh: (half * 4 + k * 2 + m, 0, 0))]
        + [pl.BlockSpec(memory_space=pl.ANY)] * len(extra),
        pl.BlockSpec((1, 8, 1, tok, width), lambda k, m, zh: (zh[0] ^ half, 0, m, 0, k)),
        jax.ShapeDtypeStruct((2, 8, batches, tok, 2 * width), BF16),
        1,
        16 * rows * 8 * tok * width,
        aliases={6: 0} if extra else {},
    )(far, *returned, table, *extra)


def weight_sum(inbound, near, other, here, so_far, scale, kind):
    _, part, width = inbound[0].shape
    quarters, ff = near.shape[1], near.shape[3]

    def body(y_ref, *refs):
        near_ref, other_ref = refs[4:6]
        out_ref, total = refs[-2:]

        @pl.when(pl.program_id(0) == 0)
        def _():
            total[...] = jnp.zeros_like(total) if so_far is None else refs[6][...]

        for d in range(4):

            @pl.when(pl.program_id(0) == d)
            def _():
                for q in range(quarters):
                    total[q] += dot(refs[d][0], near_ref[0, q], (0, 0)) + dot(
                        refs[d][1], other_ref[0, q], (0, 0)
                    )

        @pl.when(pl.program_id(0) == 3)
        def _():
            out_ref[...] = (total[...] * scale).astype(kind)

    def place(d, y):
        source = (y[0] - d) & 3
        return (source >> 1, 0, source & 1, 0)

    piece = pl.BlockSpec((1, quarters, part, ff), place)
    whole = pl.BlockSpec((quarters, width, ff), lambda d, y: (0, 0, 0))
    extra = () if so_far is None else (so_far,)
    return call(
        body,
        (4,),
        [pl.BlockSpec((2, part, width), lambda d, y: (0, 0, 0))] * 4
        + [piece, piece]
        + [whole] * len(extra),
        whole,
        jax.ShapeDtypeStruct((quarters, width, ff), kind),
        1,
        16 * part * width * quarters * ff,
        scratch=(pltpu.VMEM((quarters, width, ff), F32),),
    )(here, *inbound, near, other, *extra)


def slot_tables(expert_ids, slot_index, gate_weights, capacity, places):
    rows = expert_ids.shape[1]
    position = jnp.where(slot_index >= 0, expert_ids * capacity + slot_index, -1)
    matches = position[..., None] == jnp.arange(places, dtype=I32)
    token = jnp.arange(1, rows + 1, dtype=F32)[None, :, None, None]
    held = jnp.sum(jnp.where(matches, token, 0.0), axis=(1, 2)) - 1.0
    gate = jnp.sum(jnp.where(matches, gate_weights[..., None], 0.0), axis=(1, 2))
    return held, gate


def by(flag, a, b):
    return jnp.where(flag == 0, a, b), jnp.where(flag == 0, b, a)


def on_device(
    tokens,
    expert_ids,
    slot_index,
    gate_weights,
    up_gradient,
    up_weight,
    attention_partial,
    residual_gradient,
):
    nzl, ny, nx = (lax.axis_size(a) for a in ("zl", "y", "x"))
    zh, co, x = (lax.axis_index(a) for a in ("zh", "co", "x"))
    batches, tok, width = tokens.shape
    quarter, eighth = width // nx, width // nx // 2
    buffer_rows, ff = up_gradient.shape[3:]
    capacity = buffer_rows // (nzl * ny)
    rows = batches * buffer_rows
    far = zh.astype(I32).reshape(1)
    y = lax.axis_index("y")
    here = y.astype(I32).reshape(1)

    def gather(v):
        return lax.all_to_all(
            jnp.broadcast_to(v, (nx,) + v.shape), "x", split_axis=0, concat_axis=0, tiled=True
        ).reshape((2, 2) + v.shape)

    def along_y(parts, shape):
        moved = [
            v if d == 0 else lax.ppermute(v, "y", [(i, (i + d) % ny) for i in range(ny)])
            for d, v in enumerate(parts)
        ]
        return [v.reshape(shape) for v in moved]

    cut = up_weight.reshape(2, eighth, ff)
    mine, theirs = by(co, cut[0], cut[1])
    weight = jnp.stack(by(co, mine, lax.ppermute(theirs, "co", SWAP)))

    r = jnp.arange(rows, dtype=I32)
    r_batch = (r // (capacity * nzl)) % batches
    source_row = (
        (r_batch * nzl + (r // capacity) % nzl) * ny + r // (capacity * nzl * batches)
    ) * capacity + r % capacity
    order = (source_row[:, None] == r[None, :]).astype(BF16)
    hidden = dot(order, up_gradient.reshape(rows, ff), (1, 0)).astype(BF16)
    halves = hidden.reshape(2, rows // 2, ff)
    xh = x // 2
    keep, send = by(xh, halves[0], halves[1])
    taken = lax.ppermute(send, "x", [(i, (i + 2) % nx) for i in range(nx)])
    taken, weight = lax.optimization_barrier((taken, weight))
    stay, leave = by(xh ^ zh, keep, taken)
    crossed = lax.ppermute(leave, "zh", SWAP)
    near = gather(stay)

    expert_ids, slot_index, gate_weights, send = lax.optimization_barrier(
        (expert_ids, slot_index, gate_weights, send)
    )
    held, gate = slot_tables(expert_ids, slot_index, gate_weights, capacity, nzl * ny * capacity)
    high = lax.reduce_precision(gate, 8, 7)
    middle = lax.reduce_precision(gate - high, 8, 7)
    table = jnp.stack([held, high, middle, gate - high - middle])
    table = table.reshape(4, batches, nzl, 2, 2 * capacity).transpose(2, 0, 1, 3, 4)
    table = table.reshape(batches * tok, 2 * capacity).astype(BF16)
    table = jnp.pad(table, ((0, 0), (0, 64 - 2 * capacity)))

    own_part = lax.dynamic_slice_in_dim(tokens, x * quarter, quarter, 2)
    own_part = own_part.reshape(batches * tok, 2, eighth)
    mine, theirs = by(co, own_part[:, 0], own_part[:, 1])
    theirs = lax.ppermute(jnp.concatenate([theirs, table], axis=1), "co", SWAP)
    line = jnp.concatenate([mine, theirs[:, :eighth], table, theirs[:, eighth:]], axis=1)
    line, stay = lax.optimization_barrier((line, stay))
    line = lax.all_gather(line, ("zh", "zl"), axis=0, tiled=True)

    split = (2, batches, nzl * capacity, eighth)
    near, crossed = lax.optimization_barrier((near, crossed))
    near_other = lax.ppermute(near, "co", SWAP)
    back = rows_back(near, near_other, weight, here)
    wide = gather(crossed)
    wide, back = lax.optimization_barrier((wide, along_y(back, split)))
    wide_other = lax.ppermute(wide, "co", SWAP)
    wide_back = rows_back(wide, wide_other, weight, here)

    column = lax.dynamic_slice(
        line.reshape(2 * nzl, batches * tok, -1),
        (0, lax.axis_index("zl") * 16, quarter),
        (2 * nzl, 16, 128),
    ).reshape(2, nzl, 4, batches, 2, 2, 64)[..., : 2 * capacity]
    column = jnp.where(zh == 0, column, column[::-1]).astype(F32)
    column = column.reshape(2, nzl, 4, batches, 2, 2, 2, capacity)
    column = column.transpose(2, 0, 5, 3, 4, 6, 1, 7).reshape(
        4, 4 * batches, ny, nzl, capacity
    )
    column = lax.dynamic_slice_in_dim(jnp.concatenate([column, column], axis=2), y, ny, 2)
    start = jnp.arange(nzl, dtype=F32)[:, None] * tok
    seats = jnp.where(column[0] >= 0, column[0] + start, -1.0)
    column = jnp.stack([seats, column[1] + (column[2] + column[3])])
    column = column.reshape(2, 4 * batches, buffer_rows)
    lying, standing = column.transpose(1, 0, 2), column.transpose(1, 2, 0)

    spread = combine(0, back, lying, far, tok, None)
    spread = combine(1, along_y(wide_back, split), lying, far, tok, spread)
    expert_part = lax.psum_scatter(
        spread.reshape(2 * nzl * batches * tok, quarter),
        ("zh", "zl"),
        scatter_dimension=0,
        tiled=True,
    )

    line = line.reshape(2 * nzl, batches, tok, -1)
    line, attention_partial, _ = lax.optimization_barrier((line, attention_partial, spread))
    split = (2, batches * nzl * capacity, eighth)
    inbound = along_y(pick_rows(0, line, standing, far, eighth), split)
    inbound_far = along_y(pick_rows(1, line, standing, far, eighth), split)
    total = weight_sum(inbound, near, near_other, here, None, 1.0, F32)
    total = weight_sum(inbound_far, wide, wide_other, here, total, 1.0 / (2 * SIZES[1]), BF16)
    mine, theirs = by(co, total[0], total[1])
    weight_gradient = jnp.concatenate(by(co, mine, lax.ppermute(theirs, "co", SWAP)))

    shares = attention_partial.reshape(batches * tok, nx, quarter).transpose(1, 0, 2)
    shares = lax.all_to_all(shares, "x", split_axis=0, concat_axis=0, tiled=True)
    base = residual_gradient.reshape(batches * tok, quarter).astype(F32) + jnp.sum(
        shares.astype(F32), axis=0
    )
    other = lax.ppermute(expert_part[:, eighth:], "co", SWAP)
    expert_part = jnp.concatenate(by(co, expert_part[:, :eighth], other), axis=1)
    token_gradient = (base + expert_part.astype(F32)).astype(BF16)
    return (token_gradient.reshape(batches, tok, quarter), weight_gradient[None])


def solution(mesh):
    split = Mesh(mesh.devices.reshape(SIZES), AXES)
    dp, ep, tp = ("zh", "co"), ("zl", "y"), "x"
    return jax.shard_map(
        on_device,
        mesh=split,
        in_specs=(
            P(None, dp + ep, None),
            P(None, dp + ep, None),
            P(None, dp + ep, None),
            P(None, dp + ep, None),
            P(dp, None, ep, None, tp),
            P(ep, tp, dp),
            P(tp, None, dp + ep, None),
            P(None, dp + ep, tp),
        ),
        out_specs=(P(None, dp + ep, tp), P(ep, tp, dp)),
        check_vma=False,
    )
```

```python
import jax
import jax.numpy as jnp
from jax import lax
from jax.experimental import pallas as pl
from jax.experimental.pallas import tpu as pltpu
from jax.sharding import Mesh, PartitionSpec as P

AXES = ("zh", "co", "zl", "y", "x")
SIZES = (2, 2, 8, 4, 4)
SWAP = [(0, 1), (1, 0)]
BF16, F32, I32 = jnp.bfloat16, jnp.float32, jnp.int32
VMEM = 48 * 1024 * 1024


def dot(a, b, over):
    return lax.dot_general(a, b, ((over[:1], over[1:]), ((), ())), preferred_element_type=F32)


def call(body, grid, in_specs, out_spec, out_shape, prefetch, flops, scratch=(), aliases={}):
    return pl.pallas_call(
        body,
        grid_spec=pltpu.PrefetchScalarGridSpec(
            num_scalar_prefetch=prefetch,
            grid=grid,
            in_specs=in_specs,
            out_specs=out_spec,
            scratch_shapes=scratch,
        ),
        out_shape=out_shape,
        input_output_aliases=aliases,
        compiler_params=pltpu.CompilerParams(vmem_limit_bytes=VMEM),
        cost_estimate=pl.CostEstimate(flops=flops, bytes_accessed=1 << 23, transcendentals=0),
    )


def pick_rows(half, line, table, far, width):
    batches, tok = line.shape[1:3]
    rows = table.shape[1]
    part = rows // 4

    def body(zh_ref, line_ref, table_ref, *out_refs):
        source = line_ref[...].reshape(8 * tok, width)
        seat = table_ref[0, :, 0:1].astype(I32)
        hit = seat == lax.broadcasted_iota(I32, (rows, 8 * tok), 1)
        taken = dot(jnp.where(hit, 1.0, 0.0).astype(BF16), source, (1, 0))
        taken = (taken * table_ref[0, :, 1:2]).astype(BF16)
        for d, ref in enumerate(out_refs):
            ref[0, 0] = taken[d * part : (d + 1) * part]

    return call(
        body,
        (2, batches),
        [
            pl.BlockSpec((8, 1, tok, width), lambda k, m, zh: (zh[0] ^ half, m, 0, k)),
            pl.BlockSpec((1, rows, 2), lambda k, m, zh: (half * 4 + k * 2 + m, 0, 0)),
        ],
        [pl.BlockSpec((1, 1, part, width), lambda k, m, zh: (k, m, 0, 0))] * 4,
        [jax.ShapeDtypeStruct((2, batches, part, width), BF16)] * 4,
        1,
        8 * rows * 8 * tok * width,
    )(far, line, table)


def quarters_of(part, ff, source, relative):
    def spec(q):
        def place(d, where):
            block = source(d, where)
            x = 2 * (block >> 1) + q
            if relative:
                x = (where[1] - x) & 3
            return (x, block & 1, 0)

        return pl.BlockSpec((1, part, ff), place)

    return [spec(0), spec(1)]


def rows_back(near, other, weight, where, relative):
    _, rows, ff = near.shape
    width = weight.shape[1]
    part = rows // 2

    def body(where_ref, near0, near1, other0, other1, weight_ref, out_ref):
        for k, (first, second) in enumerate(((near0, near1), (other0, other1))):
            total = dot(first[0], weight_ref[0], (1, 1)) + dot(second[0], weight_ref[1], (1, 1))
            out_ref[0, k] = total.astype(BF16)

    pieces = quarters_of(part, ff, lambda d, where: d, relative)
    return call(
        body,
        (4,),
        pieces + pieces + [pl.BlockSpec(weight.shape, lambda d, where: (0, 0, 0))],
        pl.BlockSpec((1, 2, part, width), lambda d, where: (d, 0, 0, 0)),
        jax.ShapeDtypeStruct((4, 2, part, width), BF16),
        1,
        32 * part * ff * width,
    )(where, near, near, other, other, weight)


def combine(half, returned, table, far, tok, so_far):
    _, _, batches, part, width = returned.shape
    rows = 4 * part

    def body(zh_ref, back_ref, table_ref, *refs):
        out_ref = refs[-1]
        seat = table_ref[0, 0:1, :].astype(I32)
        hit = seat == lax.broadcasted_iota(I32, (8 * tok, rows), 0)
        gate = jnp.where(hit, table_ref[0, 1:2, :], 0.0)
        high = gate.astype(BF16)
        low = (gate - high.astype(F32)).astype(BF16)
        source = back_ref[...].reshape(rows, width)
        total = dot(high, source, (1, 0)) + dot(low, source, (1, 0))
        out_ref[...] = total.astype(BF16).reshape(out_ref.shape)

    extra = () if so_far is None else (so_far,)
    return call(
        body,
        (2, batches),
        [
            pl.BlockSpec((4, 1, 1, part, width), lambda k, m, zh: (0, k, m, 0, 0)),
            pl.BlockSpec((1, 2, rows), lambda k, m, zh: (half * 4 + k * 2 + m, 0, 0)),
        ]
        + [pl.BlockSpec(memory_space=pl.ANY)] * len(extra),
        pl.BlockSpec((1, 8, 1, tok, width), lambda k, m, zh: (zh[0] ^ half, 0, m, 0, k)),
        jax.ShapeDtypeStruct((2, 8, batches, tok, 2 * width), BF16),
        1,
        16 * rows * 8 * tok * width,
        aliases={3: 0} if extra else {},
    )(far, returned, table, *extra)


def weight_sum(inbound, near, other, where, relative, so_far, scale, kind):
    _, part, width = inbound[0].shape
    ff = near.shape[2]

    def body(where_ref, *refs):
        hidden = ((refs[4], refs[6]), (refs[5], refs[7]))
        out_ref, total = refs[-2:]

        @pl.when(pl.program_id(0) == 0)
        def _():
            total[...] = jnp.zeros_like(total) if so_far is None else refs[8][...]

        for d in range(4):

            @pl.when(pl.program_id(0) == d)
            def _():
                for q, (first, second) in enumerate(hidden):
                    total[q] += dot(refs[d][0], first[0], (0, 0)) + dot(
                        refs[d][1], second[0], (0, 0)
                    )

        @pl.when(pl.program_id(0) == 3)
        def _():
            out_ref[...] = (total[...] * scale).astype(kind)

    pieces = quarters_of(part, ff, lambda d, where: (where[0] - d) & 3, relative)
    whole = pl.BlockSpec((2, width, ff), lambda d, where: (0, 0, 0))
    extra = () if so_far is None else (so_far,)
    return call(
        body,
        (4,),
        [pl.BlockSpec((2, part, width), lambda d, where: (0, 0, 0))] * 4
        + pieces
        + pieces
        + [whole] * len(extra),
        whole,
        jax.ShapeDtypeStruct((2, width, ff), kind),
        1,
        32 * part * width * ff,
        scratch=(pltpu.VMEM((2, width, ff), F32),),
    )(where, *inbound, near, near, other, other, *extra)


def slot_tables(expert_ids, slot_index, gate_weights, capacity, places):
    rows = expert_ids.shape[1]
    position = jnp.where(slot_index >= 0, expert_ids * capacity + slot_index, -1)
    matches = position[..., None] == jnp.arange(places, dtype=I32)
    token = jnp.arange(1, rows + 1, dtype=F32)[None, :, None, None]
    held = jnp.sum(jnp.where(matches, token, 0.0), axis=(1, 2)) - 1.0
    gate = jnp.sum(jnp.where(matches, gate_weights[..., None], 0.0), axis=(1, 2))
    return held, gate


def by(flag, a, b):
    return jnp.where(flag == 0, a, b), jnp.where(flag == 0, b, a)


def on_device(
    tokens,
    expert_ids,
    slot_index,
    gate_weights,
    up_gradient,
    up_weight,
    attention_partial,
    residual_gradient,
):
    nzl, ny, nx = (lax.axis_size(a) for a in ("zl", "y", "x"))
    zh, co, x = (lax.axis_index(a) for a in ("zh", "co", "x"))
    batches, tok, width = tokens.shape
    quarter, eighth = width // nx, width // nx // 2
    buffer_rows, ff = up_gradient.shape[3:]
    capacity = buffer_rows // (nzl * ny)
    rows = batches * buffer_rows
    far = zh.astype(I32).reshape(1)
    y = lax.axis_index("y")
    here = jnp.stack([y, x]).astype(I32)

    def gather(v):
        return lax.all_to_all(
            jnp.broadcast_to(v, (nx,) + v.shape), "x", split_axis=0, concat_axis=0, tiled=True
        )

    def gather_back(v):
        return [v] + [
            lax.ppermute(v, "x", [(i, (i + d) % nx) for i in range(nx)]) for d in (1, 2, 3)
        ]

    def swap_y(v):
        shape = v.shape
        v = v.reshape(ny, -1, shape[-1])
        v = lax.all_to_all(v, "y", split_axis=0, concat_axis=0, tiled=True)
        return v.reshape(4, 2, batches, nzl * capacity, eighth)

    def along_y(parts, shape):
        moved = [
            v if d == 0 else lax.ppermute(v, "y", [(i, (i + d) % ny) for i in range(ny)])
            for d, v in enumerate(parts)
        ]
        return [v.reshape(shape) for v in moved]

    r = jnp.arange(rows, dtype=I32)
    r_batch = (r // (capacity * nzl)) % batches
    source_row = (
        (r_batch * nzl + (r // capacity) % nzl) * ny + r // (capacity * nzl * batches)
    ) * capacity + r % capacity
    order = (source_row[:, None] == r[None, :]).astype(BF16)
    hidden = dot(order, up_gradient.reshape(rows, ff), (1, 0)).astype(BF16)
    halves = hidden.reshape(2, rows // 2, ff)
    xh = x // 2
    keep, send = by(xh, halves[0], halves[1])
    taken = lax.ppermute(send, "x", [(i, (i + 2) % nx) for i in range(nx)])
    stay, leave = by(xh ^ zh, keep, taken)
    crossed = lax.ppermute(leave, "zh", SWAP)
    near = gather(stay)

    cut = up_weight.reshape(2, eighth, ff)
    mine, theirs = by(co, cut[0], cut[1])
    weight = jnp.stack(by(co, mine, lax.ppermute(theirs, "co", SWAP)))

    expert_ids, slot_index, gate_weights, send = lax.optimization_barrier(
        (expert_ids, slot_index, gate_weights, send)
    )
    held, gate = slot_tables(expert_ids, slot_index, gate_weights, capacity, nzl * ny * capacity)
    high = lax.reduce_precision(gate, 8, 7)
    middle = lax.reduce_precision(gate - high, 8, 7)
    table = jnp.stack([held, high, middle, gate - high - middle])
    table = table.reshape(4, batches, nzl, 2, 2 * capacity).transpose(2, 0, 1, 3, 4)
    table = table.reshape(batches * tok, 2 * capacity).astype(BF16)
    table = jnp.pad(table, ((0, 0), (0, 64 - 2 * capacity)))

    own_part = lax.dynamic_slice_in_dim(tokens, x * quarter, quarter, 2)
    own_part = own_part.reshape(batches * tok, 2, eighth)
    mine, theirs = by(co, own_part[:, 0], own_part[:, 1])
    theirs = lax.ppermute(jnp.concatenate([theirs, table], axis=1), "co", SWAP)
    line = jnp.concatenate([mine, theirs[:, :eighth], table, theirs[:, eighth:]], axis=1)
    line, stay = lax.optimization_barrier((line, stay))
    line = lax.all_gather(line, ("zh", "zl"), axis=0, tiled=True)

    near, crossed = lax.optimization_barrier((near, crossed))
    near_other = lax.ppermute(near, "co", SWAP)
    back = rows_back(near, near_other, weight, here, False)
    *wide, _ = lax.optimization_barrier((*gather_back(crossed), back))
    back = swap_y(back)
    wide = jnp.stack(wide)
    wide_other = lax.ppermute(wide, "co", SWAP)
    wide_back = rows_back(wide, wide_other, weight, here, True)
    wide_back, back = lax.optimization_barrier((wide_back, back))
    wide_back = swap_y(wide_back)

    column = lax.dynamic_slice(
        line.reshape(2 * nzl, batches * tok, -1),
        (0, lax.axis_index("zl") * 16, quarter),
        (2 * nzl, 16, 128),
    ).reshape(2, nzl, 4, batches, 2, 2, 64)[..., : 2 * capacity]
    column = jnp.where(zh == 0, column, column[::-1]).astype(F32)
    column = column.reshape(2, nzl, 4, batches, 2, 2, 2, capacity)
    column = column.transpose(2, 0, 5, 3, 4, 6, 1, 7).reshape(
        4, 4 * batches, ny, nzl, capacity
    )
    start = jnp.arange(nzl, dtype=F32)[:, None] * tok
    seats = jnp.where(column[0] >= 0, column[0] + start, -1.0)
    column = jnp.stack([seats, column[1] + (column[2] + column[3])])
    lying = column.reshape(2, 4 * batches, buffer_rows).transpose(1, 0, 2)
    column = lax.dynamic_slice_in_dim(jnp.concatenate([column, column], axis=2), y, ny, 2)
    standing = column.reshape(2, 4 * batches, buffer_rows).transpose(1, 2, 0)

    spread = combine(0, back, lying, far, tok, None)
    spread = combine(1, wide_back, lying, far, tok, spread)
    expert_part = lax.psum_scatter(
        spread.reshape(2 * nzl * batches * tok, quarter),
        ("zh", "zl"),
        scatter_dimension=0,
        tiled=True,
    )

    line = line.reshape(2 * nzl, batches, tok, -1)
    line, attention_partial, _ = lax.optimization_barrier((line, attention_partial, spread))
    split = (2, batches * nzl * capacity, eighth)
    inbound = along_y(pick_rows(0, line, standing, far, eighth), split)
    inbound_far = along_y(pick_rows(1, line, standing, far, eighth), split)
    total = weight_sum(inbound, near, near_other, here, False, None, 1.0, F32)
    total = weight_sum(
        inbound_far, wide, wide_other, here, True, total, 1.0 / (2 * SIZES[1]), BF16
    )
    mine, theirs = by(co, total[0], total[1])
    weight_gradient = jnp.concatenate(by(co, mine, lax.ppermute(theirs, "co", SWAP)))

    shares = attention_partial.reshape(batches * tok, nx, quarter).transpose(1, 0, 2)
    shares = lax.all_to_all(shares, "x", split_axis=0, concat_axis=0, tiled=True)
    base = residual_gradient.reshape(batches * tok, quarter).astype(F32) + jnp.sum(
        shares.astype(F32), axis=0
    )
    other = lax.ppermute(expert_part[:, eighth:], "co", SWAP)
    expert_part = jnp.concatenate(by(co, expert_part[:, :eighth], other), axis=1)
    token_gradient = (base + expert_part.astype(F32)).astype(BF16)
    return (token_gradient.reshape(batches, tok, quarter), weight_gradient[None])


def solution(mesh):
    split = Mesh(mesh.devices.reshape(SIZES), AXES)
    dp, ep, tp = ("zh", "co"), ("zl", "y"), "x"
    return jax.shard_map(
        on_device,
        mesh=split,
        in_specs=(
            P(None, dp + ep, None),
            P(None, dp + ep, None),
            P(None, dp + ep, None),
            P(None, dp + ep, None),
            P(dp, None, ep, None, tp),
            P(ep, tp, dp),
            P(tp, None, dp + ep, None),
            P(None, dp + ep, tp),
        ),
        out_specs=(P(None, dp + ep, tp), P(ep, tp, dp)),
        check_vma=False,
    )
```

```python
import jax
import jax.numpy as jnp
from jax import lax
from jax.experimental import pallas as pl
from jax.experimental.pallas import tpu as pltpu
from jax.sharding import Mesh, PartitionSpec as P

AXES = ("zh", "co", "zl", "y", "x")
SIZES = (2, 2, 8, 4, 4)
SWAP = [(0, 1), (1, 0)]
BF16, F32, I32 = jnp.bfloat16, jnp.float32, jnp.int32
VMEM = 48 * 1024 * 1024


def dot(a, b, over):
    return lax.dot_general(a, b, ((over[:1], over[1:]), ((), ())), preferred_element_type=F32)


def call(body, grid, in_specs, out_spec, out_shape, prefetch, flops, scratch=(), aliases={}):
    return pl.pallas_call(
        body,
        grid_spec=pltpu.PrefetchScalarGridSpec(
            num_scalar_prefetch=prefetch,
            grid=grid,
            in_specs=in_specs,
            out_specs=out_spec,
            scratch_shapes=scratch,
        ),
        out_shape=out_shape,
        input_output_aliases=aliases,
        compiler_params=pltpu.CompilerParams(vmem_limit_bytes=VMEM),
        cost_estimate=pl.CostEstimate(flops=flops, bytes_accessed=1 << 23, transcendentals=0),
    )


def pick_rows(half, line, table, far, width):
    batches, tok = line.shape[1:3]
    rows = table.shape[1]
    part = rows // 4

    def body(zh_ref, line_ref, table_ref, *out_refs):
        source = line_ref[...].reshape(8 * tok, width)
        seat = table_ref[0, :, 0:1].astype(I32)
        hit = seat == lax.broadcasted_iota(I32, (rows, 8 * tok), 1)
        taken = dot(jnp.where(hit, 1.0, 0.0).astype(BF16), source, (1, 0))
        taken = (taken * table_ref[0, :, 1:2]).astype(BF16)
        for d, ref in enumerate(out_refs):
            ref[0, 0] = taken[d * part : (d + 1) * part]

    return call(
        body,
        (2, batches),
        [
            pl.BlockSpec((8, 1, tok, width), lambda k, m, zh: (zh[0] ^ half, m, 0, k)),
            pl.BlockSpec((1, rows, 2), lambda k, m, zh: (half * 4 + k * 2 + m, 0, 0)),
        ],
        [pl.BlockSpec((1, 1, part, width), lambda k, m, zh: (k, m, 0, 0))] * 4,
        [jax.ShapeDtypeStruct((2, batches, part, width), BF16)] * 4,
        1,
        8 * rows * 8 * tok * width,
    )(far, line, table)


def quarters_of(part, ff, source, relative):
    def spec(q):
        def place(d, where):
            block = source(d, where)
            x = 2 * (block >> 1) + q
            if relative:
                x = (where[1] - x) & 3
            return (x, block & 1, 0)

        return pl.BlockSpec((1, part, ff), place)

    return [spec(0), spec(1)]


def rows_back(near, other, weight, where, relative):
    _, rows, ff = near.shape
    width = weight.shape[1]
    part = rows // 2

    def body(where_ref, near0, near1, other0, other1, weight_ref, out_ref):
        for k, (first, second) in enumerate(((near0, near1), (other0, other1))):
            total = dot(first[0], weight_ref[0], (1, 1)) + dot(second[0], weight_ref[1], (1, 1))
            out_ref[0, k] = total.astype(BF16)

    pieces = quarters_of(part, ff, lambda d, where: d, relative)
    return call(
        body,
        (4,),
        pieces + pieces + [pl.BlockSpec(weight.shape, lambda d, where: (0, 0, 0))],
        pl.BlockSpec((1, 2, part, width), lambda d, where: (d, 0, 0, 0)),
        jax.ShapeDtypeStruct((4, 2, part, width), BF16),
        1,
        32 * part * ff * width,
    )(where, near, near, other, other, weight)


def rows_away(near, other, weight, where):
    _, rows, ff = near.shape
    width = weight.shape[1]
    part = rows // 2

    def body(where_ref, near0, near1, other0, other1, weight_ref, *out_refs):
        for d, out_ref in enumerate(out_refs):

            @pl.when(pl.program_id(0) == d)
            def _():
                for k, (first, second) in enumerate(((near0, near1), (other0, other1))):
                    total = dot(first[0], weight_ref[0], (1, 1))
                    total += dot(second[0], weight_ref[1], (1, 1))
                    out_ref[k] = total.astype(BF16)

    pieces = quarters_of(part, ff, lambda d, where: (where[0] + d) & 3, True)
    return call(
        body,
        (4,),
        pieces + pieces + [pl.BlockSpec(weight.shape, lambda d, where: (0, 0, 0))],
        [pl.BlockSpec((2, part, width), lambda d, where: (0, 0, 0))] * 4,
        [jax.ShapeDtypeStruct((2, part, width), BF16)] * 4,
        1,
        32 * part * ff * width,
    )(where, near, near, other, other, weight)


def combine(half, returned, table, far, tok, so_far):
    _, _, batches, part, width = returned.shape
    rows = 4 * part

    def body(zh_ref, back_ref, table_ref, *refs):
        out_ref = refs[-1]
        seat = table_ref[0, 0:1, :].astype(I32)
        hit = seat == lax.broadcasted_iota(I32, (8 * tok, rows), 0)
        gate = jnp.where(hit, table_ref[0, 1:2, :], 0.0)
        high = gate.astype(BF16)
        low = (gate - high.astype(F32)).astype(BF16)
        source = back_ref[...].reshape(rows, width)
        total = dot(high, source, (1, 0)) + dot(low, source, (1, 0))
        out_ref[...] = total.astype(BF16).reshape(out_ref.shape)

    extra = () if so_far is None else (so_far,)
    return call(
        body,
        (2, batches),
        [
            pl.BlockSpec((4, 1, 1, part, width), lambda k, m, zh: (0, k, m, 0, 0)),
            pl.BlockSpec((1, 2, rows), lambda k, m, zh: (half * 4 + k * 2 + m, 0, 0)),
        ]
        + [pl.BlockSpec(memory_space=pl.ANY)] * len(extra),
        pl.BlockSpec((1, 8, 1, tok, width), lambda k, m, zh: (zh[0] ^ half, 0, m, 0, k)),
        jax.ShapeDtypeStruct((2, 8, batches, tok, 2 * width), BF16),
        1,
        16 * rows * 8 * tok * width,
        aliases={3: 0} if extra else {},
    )(far, returned, table, *extra)


def combine_parts(half, returned, table, far, tok, so_far):
    returned = [returned[d] for d in (0, 3, 2, 1)]
    _, batches, part, width = returned[0].shape
    rows = 4 * part

    def body(zh_ref, *refs):
        out_ref, table_ref = refs[-1], refs[4]
        seat = table_ref[0, 0:1, :].astype(I32)
        hit = seat == lax.broadcasted_iota(I32, (8 * tok, rows), 0)
        gate = jnp.where(hit, table_ref[0, 1:2, :], 0.0)
        high = gate.astype(BF16)
        low = (gate - high.astype(F32)).astype(BF16)
        source = jnp.concatenate([ref[0, 0] for ref in refs[:4]], axis=0)
        total = dot(high, source, (1, 0)) + dot(low, source, (1, 0))
        out_ref[...] = total.astype(BF16).reshape(out_ref.shape)

    extra = () if so_far is None else (so_far,)
    return call(
        body,
        (2, batches),
        [pl.BlockSpec((1, 1, part, width), lambda k, m, zh: (k, m, 0, 0))] * 4
        + [pl.BlockSpec((1, 2, rows), lambda k, m, zh: (half * 4 + k * 2 + m, 0, 0))]
        + [pl.BlockSpec(memory_space=pl.ANY)] * len(extra),
        pl.BlockSpec((1, 8, 1, tok, width), lambda k, m, zh: (zh[0] ^ half, 0, m, 0, k)),
        jax.ShapeDtypeStruct((2, 8, batches, tok, 2 * width), BF16),
        1,
        16 * rows * 8 * tok * width,
        aliases={6: 0} if extra else {},
    )(far, *returned, table, *extra)


def weight_sum(inbound, near, other, where, relative, so_far, scale, kind):
    _, part, width = inbound[0].shape
    ff = near.shape[2]

    def body(where_ref, *refs):
        hidden = ((refs[4], refs[6]), (refs[5], refs[7]))
        out_ref, total = refs[-2:]

        @pl.when(pl.program_id(0) == 0)
        def _():
            total[...] = jnp.zeros_like(total) if so_far is None else refs[8][...]

        for d in range(4):

            @pl.when(pl.program_id(0) == d)
            def _():
                for q, (first, second) in enumerate(hidden):
                    total[q] += dot(refs[d][0], first[0], (0, 0)) + dot(
                        refs[d][1], second[0], (0, 0)
                    )

        @pl.when(pl.program_id(0) == 3)
        def _():
            out_ref[...] = (total[...] * scale).astype(kind)

    pieces = quarters_of(part, ff, lambda d, where: (where[0] - d) & 3, relative)
    whole = pl.BlockSpec((2, width, ff), lambda d, where: (0, 0, 0))
    extra = () if so_far is None else (so_far,)
    return call(
        body,
        (4,),
        [pl.BlockSpec((2, part, width), lambda d, where: (0, 0, 0))] * 4
        + pieces
        + pieces
        + [whole] * len(extra),
        whole,
        jax.ShapeDtypeStruct((2, width, ff), kind),
        1,
        32 * part * width * ff,
        scratch=(pltpu.VMEM((2, width, ff), F32),),
    )(where, *inbound, near, near, other, other, *extra)


def slot_tables(expert_ids, slot_index, gate_weights, capacity, places):
    rows = expert_ids.shape[1]
    position = jnp.where(slot_index >= 0, expert_ids * capacity + slot_index, -1)
    matches = position[..., None] == jnp.arange(places, dtype=I32)
    token = jnp.arange(1, rows + 1, dtype=F32)[None, :, None, None]
    held = jnp.sum(jnp.where(matches, token, 0.0), axis=(1, 2)) - 1.0
    gate = jnp.sum(jnp.where(matches, gate_weights[..., None], 0.0), axis=(1, 2))
    return held, gate


def by(flag, a, b):
    return jnp.where(flag == 0, a, b), jnp.where(flag == 0, b, a)


def on_device(
    tokens,
    expert_ids,
    slot_index,
    gate_weights,
    up_gradient,
    up_weight,
    attention_partial,
    residual_gradient,
):
    nzl, ny, nx = (lax.axis_size(a) for a in ("zl", "y", "x"))
    zh, co, x = (lax.axis_index(a) for a in ("zh", "co", "x"))
    batches, tok, width = tokens.shape
    quarter, eighth = width // nx, width // nx // 2
    buffer_rows, ff = up_gradient.shape[3:]
    capacity = buffer_rows // (nzl * ny)
    rows = batches * buffer_rows
    far = zh.astype(I32).reshape(1)
    y = lax.axis_index("y")
    here = jnp.stack([y, x]).astype(I32)

    def gather(v):
        return lax.all_to_all(
            jnp.broadcast_to(v, (nx,) + v.shape), "x", split_axis=0, concat_axis=0, tiled=True
        )

    def gather_back(v):
        return [v] + [
            lax.ppermute(v, "x", [(i, (i + d) % nx) for i in range(nx)]) for d in (1, 2, 3)
        ]

    def swap_y(v):
        shape = v.shape
        v = v.reshape(ny, -1, shape[-1])
        v = lax.all_to_all(v, "y", split_axis=0, concat_axis=0, tiled=True)
        return v.reshape(4, 2, batches, nzl * capacity, eighth)

    def along_y(parts, shape):
        moved = [
            v if d == 0 else lax.ppermute(v, "y", [(i, (i + d) % ny) for i in range(ny)])
            for d, v in enumerate(parts)
        ]
        return [v.reshape(shape) for v in moved]

    r = jnp.arange(rows, dtype=I32)
    r_batch = (r // (capacity * nzl)) % batches
    source_row = (
        (r_batch * nzl + (r // capacity) % nzl) * ny + r // (capacity * nzl * batches)
    ) * capacity + r % capacity
    order = (source_row[:, None] == r[None, :]).astype(BF16)
    hidden = dot(order, up_gradient.reshape(rows, ff), (1, 0)).astype(BF16)
    halves = hidden.reshape(2, rows // 2, ff)
    xh = x // 2
    keep, send = by(xh, halves[0], halves[1])
    taken = lax.ppermute(send, "x", [(i, (i + 2) % nx) for i in range(nx)])
    stay, leave = by(xh ^ zh, keep, taken)
    crossed = lax.ppermute(leave, "zh", SWAP)
    near = gather(stay)

    cut = up_weight.reshape(2, eighth, ff)
    mine, theirs = by(co, cut[0], cut[1])
    weight = jnp.stack(by(co, mine, lax.ppermute(theirs, "co", SWAP)))

    expert_ids, slot_index, gate_weights, send = lax.optimization_barrier(
        (expert_ids, slot_index, gate_weights, send)
    )
    held, gate = slot_tables(expert_ids, slot_index, gate_weights, capacity, nzl * ny * capacity)
    high = lax.reduce_precision(gate, 8, 7)
    middle = lax.reduce_precision(gate - high, 8, 7)
    table = jnp.stack([held, high, middle, gate - high - middle])
    table = table.reshape(4, batches, nzl, 2, 2 * capacity).transpose(2, 0, 1, 3, 4)
    table = table.reshape(batches * tok, 2 * capacity).astype(BF16)
    table = jnp.pad(table, ((0, 0), (0, 64 - 2 * capacity)))

    own_part = lax.dynamic_slice_in_dim(tokens, x * quarter, quarter, 2)
    own_part = own_part.reshape(batches * tok, 2, eighth)
    mine, theirs = by(co, own_part[:, 0], own_part[:, 1])
    theirs = lax.ppermute(jnp.concatenate([theirs, table], axis=1), "co", SWAP)
    line = jnp.concatenate([mine, theirs[:, :eighth], table, theirs[:, eighth:]], axis=1)
    line, stay = lax.optimization_barrier((line, stay))
    line = lax.all_gather(line, ("zh", "zl"), axis=0, tiled=True)

    near, crossed = lax.optimization_barrier((near, crossed))
    near_other = lax.ppermute(near, "co", SWAP)
    back = rows_back(near, near_other, weight, here, False)
    *wide, _ = lax.optimization_barrier((*gather_back(crossed), back))
    back = swap_y(back)
    wide = jnp.stack(wide)
    wide_other = lax.ppermute(wide, "co", SWAP)
    split = (2, batches, nzl * capacity, eighth)
    wide_back = along_y(rows_away(wide, wide_other, weight, here), split)

    column = lax.dynamic_slice(
        line.reshape(2 * nzl, batches * tok, -1),
        (0, lax.axis_index("zl") * 16, quarter),
        (2 * nzl, 16, 128),
    ).reshape(2, nzl, 4, batches, 2, 2, 64)[..., : 2 * capacity]
    column = jnp.where(zh == 0, column, column[::-1]).astype(F32)
    column = column.reshape(2, nzl, 4, batches, 2, 2, 2, capacity)
    column = column.transpose(2, 0, 5, 3, 4, 6, 1, 7).reshape(
        4, 4 * batches, ny, nzl, capacity
    )
    start = jnp.arange(nzl, dtype=F32)[:, None] * tok
    seats = jnp.where(column[0] >= 0, column[0] + start, -1.0)
    column = jnp.stack([seats, column[1] + (column[2] + column[3])])
    lying = column.reshape(2, 4 * batches, buffer_rows).transpose(1, 0, 2)
    column = lax.dynamic_slice_in_dim(jnp.concatenate([column, column], axis=2), y, ny, 2)
    column = column.reshape(2, 4 * batches, buffer_rows)
    turned, standing = column.transpose(1, 0, 2), column.transpose(1, 2, 0)

    spread = combine(0, back, lying, far, tok, None)
    spread = combine_parts(1, wide_back, turned, far, tok, spread)
    expert_part = lax.psum_scatter(
        spread.reshape(2 * nzl * batches * tok, quarter),
        ("zh", "zl"),
        scatter_dimension=0,
        tiled=True,
    )

    line = line.reshape(2 * nzl, batches, tok, -1)
    line, attention_partial, _ = lax.optimization_barrier((line, attention_partial, spread))
    split = (2, batches * nzl * capacity, eighth)
    inbound = along_y(pick_rows(0, line, standing, far, eighth), split)
    inbound_far = along_y(pick_rows(1, line, standing, far, eighth), split)
    total = weight_sum(inbound, near, near_other, here, False, None, 1.0, F32)
    total = weight_sum(
        inbound_far, wide, wide_other, here, True, total, 1.0 / (2 * SIZES[1]), BF16
    )
    mine, theirs = by(co, total[0], total[1])
    weight_gradient = jnp.concatenate(by(co, mine, lax.ppermute(theirs, "co", SWAP)))

    shares = attention_partial.reshape(batches * tok, nx, quarter).transpose(1, 0, 2)
    shares = lax.all_to_all(shares, "x", split_axis=0, concat_axis=0, tiled=True)
    base = residual_gradient.reshape(batches * tok, quarter).astype(F32) + jnp.sum(
        shares.astype(F32), axis=0
    )
    other = lax.ppermute(expert_part[:, eighth:], "co", SWAP)
    expert_part = jnp.concatenate(by(co, expert_part[:, :eighth], other), axis=1)
    token_gradient = (base + expert_part.astype(F32)).astype(BF16)
    return (token_gradient.reshape(batches, tok, quarter), weight_gradient[None])


def solution(mesh):
    split = Mesh(mesh.devices.reshape(SIZES), AXES)
    dp, ep, tp = ("zh", "co"), ("zl", "y"), "x"
    return jax.shard_map(
        on_device,
        mesh=split,
        in_specs=(
            P(None, dp + ep, None),
            P(None, dp + ep, None),
            P(None, dp + ep, None),
            P(None, dp + ep, None),
            P(dp, None, ep, None, tp),
            P(ep, tp, dp),
            P(tp, None, dp + ep, None),
            P(None, dp + ep, tp),
        ),
        out_specs=(P(None, dp + ep, tp), P(ep, tp, dp)),
        check_vma=False,
    )
```

```python
import jax
import jax.numpy as jnp
from jax import lax
from jax.experimental import pallas as pl
from jax.experimental.pallas import tpu as pltpu
from jax.sharding import Mesh, PartitionSpec as P

AXES = ("zh", "co", "zl", "y", "x")
SIZES = (2, 2, 8, 4, 4)
SWAP = [(0, 1), (1, 0)]
BF16, F32, I32 = jnp.bfloat16, jnp.float32, jnp.int32
VMEM = 48 * 1024 * 1024


def dot(a, b, over):
    return lax.dot_general(a, b, ((over[:1], over[1:]), ((), ())), preferred_element_type=F32)


def call(body, grid, in_specs, out_spec, out_shape, prefetch, flops, scratch=(), aliases={}):
    return pl.pallas_call(
        body,
        grid_spec=pltpu.PrefetchScalarGridSpec(
            num_scalar_prefetch=prefetch,
            grid=grid,
            in_specs=in_specs,
            out_specs=out_spec,
            scratch_shapes=scratch,
        ),
        out_shape=out_shape,
        input_output_aliases=aliases,
        compiler_params=pltpu.CompilerParams(vmem_limit_bytes=VMEM),
        cost_estimate=pl.CostEstimate(flops=flops, bytes_accessed=1 << 23, transcendentals=0),
    )


def pick_rows(half, line, table, far, width):
    batches, tok = line.shape[1:3]
    rows = table.shape[1]
    part = rows // 4

    def body(zh_ref, line_ref, table_ref, *out_refs):
        source = line_ref[...].reshape(8 * tok, width)
        seat = table_ref[0, :, 0:1].astype(I32)
        hit = seat == lax.broadcasted_iota(I32, (rows, 8 * tok), 1)
        taken = dot(jnp.where(hit, 1.0, 0.0).astype(BF16), source, (1, 0))
        taken = (taken * table_ref[0, :, 1:2]).astype(BF16)
        for d, ref in enumerate(out_refs):
            ref[0, 0] = taken[d * part : (d + 1) * part]

    return call(
        body,
        (2, batches),
        [
            pl.BlockSpec((8, 1, tok, width), lambda k, m, zh: (zh[0] ^ half, m, 0, k)),
            pl.BlockSpec((1, rows, 2), lambda k, m, zh: (half * 4 + k * 2 + m, 0, 0)),
        ],
        [pl.BlockSpec((1, 1, part, width), lambda k, m, zh: (k, m, 0, 0))] * 4,
        [jax.ShapeDtypeStruct((2, batches, part, width), BF16)] * 4,
        1,
        8 * rows * 8 * tok * width,
    )(far, line, table)


def quarters_of(part, ff, source, relative):
    def spec(q):
        def place(d, where):
            block = source(d, where)
            x = 2 * (block >> 1) + q
            if relative:
                x = (where[1] - x) & 3
            return (x, block & 1, 0)

        return pl.BlockSpec((1, part, ff), place)

    return [spec(0), spec(1)]


def rows_back(near, other, weight, where, relative):
    _, rows, ff = near.shape
    width = weight.shape[1]
    part = rows // 2

    def body(where_ref, near0, near1, other0, other1, weight_ref, out_ref):
        for k, (first, second) in enumerate(((near0, near1), (other0, other1))):
            total = dot(first[0], weight_ref[0], (1, 1)) + dot(second[0], weight_ref[1], (1, 1))
            out_ref[0, k] = total.astype(BF16)

    pieces = quarters_of(part, ff, lambda d, where: d, relative)
    return call(
        body,
        (4,),
        pieces + pieces + [pl.BlockSpec(weight.shape, lambda d, where: (0, 0, 0))],
        pl.BlockSpec((1, 2, part, width), lambda d, where: (d, 0, 0, 0)),
        jax.ShapeDtypeStruct((4, 2, part, width), BF16),
        1,
        32 * part * ff * width,
    )(where, near, near, other, other, weight)


def rows_away(near, other, weight, where):
    _, rows, ff = near.shape
    width = weight.shape[1]
    part = rows // 2

    def body(where_ref, near0, near1, other0, other1, weight_ref, *out_refs):
        for d, out_ref in enumerate(out_refs):

            @pl.when(pl.program_id(0) == d)
            def _():
                for k, (first, second) in enumerate(((near0, near1), (other0, other1))):
                    total = dot(first[0], weight_ref[0], (1, 1))
                    total += dot(second[0], weight_ref[1], (1, 1))
                    out_ref[k] = total.astype(BF16)

    pieces = quarters_of(part, ff, lambda d, where: (where[0] + d) & 3, True)
    return call(
        body,
        (4,),
        pieces + pieces + [pl.BlockSpec(weight.shape, lambda d, where: (0, 0, 0))],
        [pl.BlockSpec((2, part, width), lambda d, where: (0, 0, 0))] * 4,
        [jax.ShapeDtypeStruct((2, part, width), BF16)] * 4,
        1,
        32 * part * ff * width,
    )(where, near, near, other, other, weight)


def combine(half, returned, table, far, tok, so_far):
    _, _, batches, part, width = returned.shape
    rows = 4 * part

    def body(zh_ref, back_ref, table_ref, *refs):
        out_ref = refs[-1]
        seat = table_ref[0, 0:1, :].astype(I32)
        hit = seat == lax.broadcasted_iota(I32, (8 * tok, rows), 0)
        gate = jnp.where(hit, table_ref[0, 1:2, :], 0.0)
        high = gate.astype(BF16)
        low = (gate - high.astype(F32)).astype(BF16)
        source = back_ref[...].reshape(rows, width)
        total = dot(high, source, (1, 0)) + dot(low, source, (1, 0))
        out_ref[...] = total.astype(BF16).reshape(out_ref.shape)

    extra = () if so_far is None else (so_far,)
    return call(
        body,
        (2, batches),
        [
            pl.BlockSpec((4, 1, 1, part, width), lambda k, m, zh: (0, k, m, 0, 0)),
            pl.BlockSpec((1, 2, rows), lambda k, m, zh: (half * 4 + k * 2 + m, 0, 0)),
        ]
        + [pl.BlockSpec(memory_space=pl.ANY)] * len(extra),
        pl.BlockSpec((1, 8, 1, tok, width), lambda k, m, zh: (zh[0] ^ half, 0, m, 0, k)),
        jax.ShapeDtypeStruct((2, 8, batches, tok, 2 * width), BF16),
        1,
        16 * rows * 8 * tok * width,
        aliases={3: 0} if extra else {},
    )(far, returned, table, *extra)


def combine_parts(half, returned, table, far, tok, so_far):
    returned = [returned[d] for d in (0, 3, 2, 1)]
    _, batches, part, width = returned[0].shape
    rows = 4 * part

    def body(zh_ref, *refs):
        out_ref, table_ref = refs[-1], refs[4]
        seat = table_ref[0, 0:1, :].astype(I32)
        hit = seat == lax.broadcasted_iota(I32, (8 * tok, rows), 0)
        gate = jnp.where(hit, table_ref[0, 1:2, :], 0.0)
        high = gate.astype(BF16)
        low = (gate - high.astype(F32)).astype(BF16)
        source = jnp.concatenate([ref[0, 0] for ref in refs[:4]], axis=0)
        total = dot(high, source, (1, 0)) + dot(low, source, (1, 0))
        out_ref[...] = total.astype(BF16).reshape(out_ref.shape)

    extra = () if so_far is None else (so_far,)
    return call(
        body,
        (2, batches),
        [pl.BlockSpec((1, 1, part, width), lambda k, m, zh: (k, m, 0, 0))] * 4
        + [pl.BlockSpec((1, 2, rows), lambda k, m, zh: (half * 4 + k * 2 + m, 0, 0))]
        + [pl.BlockSpec(memory_space=pl.ANY)] * len(extra),
        pl.BlockSpec((1, 8, 1, tok, width), lambda k, m, zh: (zh[0] ^ half, 0, m, 0, k)),
        jax.ShapeDtypeStruct((2, 8, batches, tok, 2 * width), BF16),
        1,
        16 * rows * 8 * tok * width,
        aliases={6: 0} if extra else {},
    )(far, *returned, table, *extra)


def weight_sum(inbound, near, other, where, relative, so_far, scale, kind):
    _, part, width = inbound[0].shape
    ff = near.shape[2]

    def body(where_ref, *refs):
        hidden = ((refs[4], refs[6]), (refs[5], refs[7]))
        out_ref, total = refs[-2:]

        @pl.when(pl.program_id(0) == 0)
        def _():
            total[...] = jnp.zeros_like(total) if so_far is None else refs[8][...]

        for d in range(4):

            @pl.when(pl.program_id(0) == d)
            def _():
                for q, (first, second) in enumerate(hidden):
                    total[q] += dot(refs[d][0], first[0], (0, 0)) + dot(
                        refs[d][1], second[0], (0, 0)
                    )

        @pl.when(pl.program_id(0) == 3)
        def _():
            out_ref[...] = (total[...] * scale).astype(kind)

    pieces = quarters_of(part, ff, lambda d, where: (where[0] - d) & 3, relative)
    whole = pl.BlockSpec((2, width, ff), lambda d, where: (0, 0, 0))
    extra = () if so_far is None else (so_far,)
    return call(
        body,
        (4,),
        [pl.BlockSpec((2, part, width), lambda d, where: (0, 0, 0))] * 4
        + pieces
        + pieces
        + [whole] * len(extra),
        whole,
        jax.ShapeDtypeStruct((2, width, ff), kind),
        1,
        32 * part * width * ff,
        scratch=(pltpu.VMEM((2, width, ff), F32),),
    )(where, *inbound, near, near, other, other, *extra)


def slot_tables(expert_ids, slot_index, gate_weights, capacity, places):
    rows = expert_ids.shape[1]
    position = jnp.where(slot_index >= 0, expert_ids * capacity + slot_index, -1)
    matches = position[..., None] == jnp.arange(places, dtype=I32)
    token = jnp.arange(1, rows + 1, dtype=F32)[None, :, None, None]
    held = jnp.sum(jnp.where(matches, token, 0.0), axis=(1, 2)) - 1.0
    gate = jnp.sum(jnp.where(matches, gate_weights[..., None], 0.0), axis=(1, 2))
    return held, gate


def by(flag, a, b):
    return jnp.where(flag == 0, a, b), jnp.where(flag == 0, b, a)


def on_device(
    tokens,
    expert_ids,
    slot_index,
    gate_weights,
    up_gradient,
    up_weight,
    attention_partial,
    residual_gradient,
):
    nzl, ny, nx = (lax.axis_size(a) for a in ("zl", "y", "x"))
    zh, co, x = (lax.axis_index(a) for a in ("zh", "co", "x"))
    batches, tok, width = tokens.shape
    quarter, eighth = width // nx, width // nx // 2
    buffer_rows, ff = up_gradient.shape[3:]
    capacity = buffer_rows // (nzl * ny)
    rows = batches * buffer_rows
    far = zh.astype(I32).reshape(1)
    y = lax.axis_index("y")
    here = jnp.stack([y, x]).astype(I32)

    def gather(v):
        return lax.all_to_all(
            jnp.broadcast_to(v, (nx,) + v.shape), "x", split_axis=0, concat_axis=0, tiled=True
        )

    def gather_back(v):
        return [v] + [
            lax.ppermute(v, "x", [(i, (i + d) % nx) for i in range(nx)]) for d in (1, 2, 3)
        ]

    def swap_y(v):
        shape = v.shape
        v = v.reshape(ny, -1, shape[-1])
        v = lax.all_to_all(v, "y", split_axis=0, concat_axis=0, tiled=True)
        return v.reshape(4, 2, batches, nzl * capacity, eighth)

    def along_y(parts, shape):
        moved = [
            v if d == 0 else lax.ppermute(v, "y", [(i, (i + d) % ny) for i in range(ny)])
            for d, v in enumerate(parts)
        ]
        return [v.reshape(shape) for v in moved]

    r = jnp.arange(rows, dtype=I32)
    r_batch = (r // (capacity * nzl)) % batches
    source_row = (
        (r_batch * nzl + (r // capacity) % nzl) * ny + r // (capacity * nzl * batches)
    ) * capacity + r % capacity
    order = (source_row[:, None] == r[None, :]).astype(BF16)
    hidden = dot(order, up_gradient.reshape(rows, ff), (1, 0)).astype(BF16)
    halves = hidden.reshape(2, rows // 2, ff)
    xh = x // 2
    keep, send = by(xh, halves[0], halves[1])
    taken = lax.ppermute(send, "x", [(i, (i + 2) % nx) for i in range(nx)])
    stay, leave = by(xh ^ zh, keep, taken)
    crossed = lax.ppermute(leave, "zh", SWAP)
    near = gather(stay)

    cut = up_weight.reshape(2, eighth, ff)
    mine, theirs = by(co, cut[0], cut[1])
    weight = jnp.stack(by(co, mine, lax.ppermute(theirs, "co", SWAP)))

    expert_ids, slot_index, gate_weights, send = lax.optimization_barrier(
        (expert_ids, slot_index, gate_weights, send)
    )
    held, gate = slot_tables(expert_ids, slot_index, gate_weights, capacity, nzl * ny * capacity)
    high = lax.reduce_precision(gate, 8, 7)
    middle = lax.reduce_precision(gate - high, 8, 7)
    table = jnp.stack([held, high, middle, gate - high - middle])
    table = table.reshape(4, batches, nzl, 2, 2 * capacity).transpose(2, 0, 1, 3, 4)
    table = table.reshape(batches * tok, 2 * capacity).astype(BF16)
    table = jnp.pad(table, ((0, 0), (0, 64 - 2 * capacity)))

    own_part = lax.dynamic_slice_in_dim(tokens, x * quarter, quarter, 2)
    own_part = own_part.reshape(batches * tok, 2, eighth)
    mine, theirs = by(co, own_part[:, 0], own_part[:, 1])
    theirs = lax.ppermute(jnp.concatenate([theirs, table], axis=1), "co", SWAP)
    line = jnp.concatenate([mine, theirs[:, :eighth], table, theirs[:, eighth:]], axis=1)
    line, stay = lax.optimization_barrier((line, stay))
    line = lax.all_gather(line, ("zh", "zl"), axis=0, tiled=True)

    near, crossed, weight = lax.optimization_barrier((near, crossed, weight))
    near_other = lax.ppermute(near, "co", SWAP)
    back = rows_back(near, near_other, weight, here, False)
    *wide, _ = lax.optimization_barrier((*gather_back(crossed), back))
    back = swap_y(back)
    wide = jnp.stack(wide)
    wide_other = lax.ppermute(wide, "co", SWAP)
    split = (2, batches, nzl * capacity, eighth)
    wide_back = along_y(rows_away(wide, wide_other, weight, here), split)

    column = lax.dynamic_slice(
        line.reshape(2 * nzl, batches * tok, -1),
        (0, lax.axis_index("zl") * 16, quarter),
        (2 * nzl, 16, 128),
    ).reshape(2, nzl, 4, batches, 2, 2, 64)[..., : 2 * capacity]
    column = jnp.where(zh == 0, column, column[::-1]).astype(F32)
    column = column.reshape(2, nzl, 4, batches, 2, 2, 2, capacity)
    column = column.transpose(2, 0, 5, 3, 4, 6, 1, 7).reshape(
        4, 4 * batches, ny, nzl, capacity
    )
    start = jnp.arange(nzl, dtype=F32)[:, None] * tok
    seats = jnp.where(column[0] >= 0, column[0] + start, -1.0)
    column = jnp.stack([seats, column[1] + (column[2] + column[3])])
    lying = column.reshape(2, 4 * batches, buffer_rows).transpose(1, 0, 2)
    column = lax.dynamic_slice_in_dim(jnp.concatenate([column, column], axis=2), y, ny, 2)
    column = column.reshape(2, 4 * batches, buffer_rows)
    turned, standing = column.transpose(1, 0, 2), column.transpose(1, 2, 0)

    spread = combine(0, back, lying, far, tok, None)
    spread = combine_parts(1, wide_back, turned, far, tok, spread)
    expert_part = lax.psum_scatter(
        spread.reshape(2 * nzl * batches * tok, quarter),
        ("zh", "zl"),
        scatter_dimension=0,
        tiled=True,
    )

    line = line.reshape(2 * nzl, batches, tok, -1)
    line, attention_partial, _ = lax.optimization_barrier((line, attention_partial, spread))
    split = (2, batches * nzl * capacity, eighth)
    inbound = along_y(pick_rows(0, line, standing, far, eighth), split)
    inbound_far = along_y(pick_rows(1, line, standing, far, eighth), split)
    total = weight_sum(inbound, near, near_other, here, False, None, 1.0, F32)
    total = weight_sum(
        inbound_far, wide, wide_other, here, True, total, 1.0 / (2 * SIZES[1]), BF16
    )
    mine, theirs = by(co, total[0], total[1])
    weight_gradient = jnp.concatenate(by(co, mine, lax.ppermute(theirs, "co", SWAP)))

    shares = attention_partial.reshape(batches * tok, nx, quarter).transpose(1, 0, 2)
    shares = lax.all_to_all(shares, "x", split_axis=0, concat_axis=0, tiled=True)
    base = residual_gradient.reshape(batches * tok, quarter).astype(F32) + jnp.sum(
        shares.astype(F32), axis=0
    )
    other = lax.ppermute(expert_part[:, eighth:], "co", SWAP)
    expert_part = jnp.concatenate(by(co, expert_part[:, :eighth], other), axis=1)
    token_gradient = (base + expert_part.astype(F32)).astype(BF16)
    return (token_gradient.reshape(batches, tok, quarter), weight_gradient[None])


def solution(mesh):
    split = Mesh(mesh.devices.reshape(SIZES), AXES)
    dp, ep, tp = ("zh", "co"), ("zl", "y"), "x"
    return jax.shard_map(
        on_device,
        mesh=split,
        in_specs=(
            P(None, dp + ep, None),
            P(None, dp + ep, None),
            P(None, dp + ep, None),
            P(None, dp + ep, None),
            P(dp, None, ep, None, tp),
            P(ep, tp, dp),
            P(tp, None, dp + ep, None),
            P(None, dp + ep, tp),
        ),
        out_specs=(P(None, dp + ep, tp), P(ep, tp, dp)),
        check_vma=False,
    )
```
